256 devices in a mesh: space: 16 (over x_hi, y, core), var: 2 (over x_lo), tm: 8 (over z).
Axes of the slice: x: 4 (x_hi: 2, x_lo: 2; x = x_hi * 2 + x_lo), y: 4, z: 8, core: 2. Of those that a mesh axis runs over, the one named last changes fastest.
Arguments:
- field: bfloat16 [128, 256, 32768], P('tm', 'var', 'space'), may hold values from -6 to 6
- factor_space: bfloat16 [32768, 128], P(('space', 'var', 'tm')), may hold values from -3 to 3
- factor_level: bfloat16 [256, 128], P('var'), may hold values from -3 to 3
- factor_time: bfloat16 [128, 128], P('tm'), may hold values from -3 to 3
Outputs:
- grad_space: float32 [32768, 128], P(('space', 'var', 'tm'))
- grad_level: float32 [256, 128], P('var')
- grad_time: float32 [128, 128], P('tm')
- loss: float32 [], replicated
The draws below stay inside these ranges and needn't reach their ends.
All inputs are finite; a program needn't handle non-finite values.
Results may differ from the reference program's by a relative error of at most 0.00071.
Values may be sent and summed in bfloat16 or wider, within the bound.
A program may use at most 64 MiB of HBM per device.

```python
import jax
import jax.numpy as jnp
from jax import lax

RANK = 128
J = 256
I = 32768
K = 128


def level_of(stream_key, dims, shards, smallest, top_value):
    level, own = 1.0, jax.random.fold_in(stream_key, 6)
    for position, shards_of in shards:
        draws = jnp.exp(jax.random.uniform(jax.random.fold_in(own, position), (shards_of,), jnp.float32, smallest / len(shards), top_value / len(shards)))
        level = level * jnp.repeat(draws, dims[position] // shards_of).reshape([-1 if axis == position else 1 for axis in range(len(dims))])
    return level


def scatter_about(key, dims, deviation, limit, cuts=(), dtype=jnp.bfloat16):
    factor_of = level_of(key, dims, cuts, -0.22, 0.18) if cuts else 1.0
    result = jax.random.normal(key, dims, jnp.float32) * deviation * factor_of
    return jnp.minimum(jnp.maximum(result, -limit), limit).astype(dtype)


def setup_inputs(seed: int = 0) -> dict:
    keys = jax.random.split(jax.random.key(seed), 5)
    field = scatter_about(keys[0], (K, J, I), 1.0, 6.0, ((0, 8), (1, 2), (2, 16)))
    factor_space = scatter_about(keys[1], (I, RANK), 0.45, 3.0, ((0, 256),))
    factor_level = scatter_about(keys[2], (J, RANK), 0.45, 3.0, ((0, 2),))
    factor_time = scatter_about(keys[3], (K, RANK), 0.45, 3.0, ((0, 8),))
    return dict(field=field, factor_space=factor_space, factor_level=factor_level, factor_time=factor_time)


def reference(field, factor_space, factor_level, factor_time):
    level32 = factor_level.astype(jnp.float32)

    def step(carry, inputs):
        grad_a, grad_b, total = carry
        slab, row = inputs
        row32 = row.astype(jnp.float32)
        khatri = (level32 * row32[None, :]).astype(jnp.bfloat16)
        model = jnp.dot(khatri, factor_space.T, preferred_element_type=jnp.float32)
        misfit = model - slab.astype(jnp.float32)
        misfit_b = misfit.astype(jnp.bfloat16)
        grad_a = grad_a + jnp.dot(misfit_b.T, khatri, preferred_element_type=jnp.float32)
        project = jnp.dot(misfit_b, factor_space, preferred_element_type=jnp.float32)
        grad_b = grad_b + project * row32[None, :]
        grad_c = lax.optimization_barrier(jnp.sum(project * level32, axis=0))
        total = total + jnp.sum(misfit * misfit)
        return ((grad_a, grad_b, total), grad_c)
    start = (jnp.zeros((I, RANK), jnp.float32), jnp.zeros((J, RANK), jnp.float32), jnp.zeros((), jnp.float32))
    (grad_a, grad_b, total), grad_c = lax.scan(step, start, (field, factor_time))
    grad_space = grad_a / jnp.sqrt(jnp.float32(J * K))
    grad_level = grad_b / jnp.sqrt(jnp.float32(I * K))
    grad_time = grad_c / jnp.sqrt(jnp.float32(I * J))
    loss = 0.5 * total / jnp.float32(I * J * K)
    return (grad_space, grad_level, grad_time, loss)
```

```python
import functools

import jax
import jax.numpy as jnp
from jax import lax
from jax.experimental import pallas as pl
from jax.experimental.pallas import tpu as pltpu
from jax.sharding import PartitionSpec as P

MESH = pl.DeviceIdType.MESH
BF16, F32 = jnp.bfloat16, jnp.float32
NS, NV, NT = 16, 2, 8
CHUNK = 256


def offset_of(s):
    if isinstance(s, int):
        return (0, 4, 3, 5, 2, 6, 1, 7)[s]
    mag = 4 - s // 2
    signed = jnp.where(s % 2 == 0, mag, NT - mag)
    return jnp.where(s == 0, 0, jnp.where(s == 1, 4, signed))


def mirror(s):
    return (0, 1, 3, 2, 5, 4, 7, 6)[s]


def kernel(scales, field, s_ref, l_ref, t_ref, gs_ref, gl_ref, gt_ref, loss_ref,
           fbuf, ag, khat, khat_t, mb, proj, sq, part, xbuf, zs, zbuf,
           m1, r1, m2, r2, m3, r3, glf,
           fsem, agz_s, agz_r, agx_s, agx_r, rx_s, rx_r, rz_s, rz_r,
           p1_s, p1_r, p2_s, p2_r, p3_s, p3_r, px_s, px_r):
    sp, v, t = lax.axis_index("space"), lax.axis_index("var"), lax.axis_index("tm")
    partner = {"var": 1 - v}
    nk, nj = t_ref.shape[0], l_ref.shape[0]

    def zpeer(s):
        return lax.rem(t + offset_of(s), NT)

    def remote(src, dst, send, recv, dev):
        return pltpu.make_async_remote_copy(src_ref=src, dst_ref=dst, send_sem=send, recv_sem=recv,
                                            device_id=dev, device_id_type=MESH)

    def field_copy(s, h):
        owner = (v if h == 0 else 1 - v) * NT + lax.rem(t + offset_of(s), NT)
        cols = pl.ds(pl.multiple_of(owner * 128, 128), 128)
        return pltpu.make_async_copy(field.at[:, :, cols], fbuf.at[s, :, :, pl.ds(h * 128, 128)], fsem.at[s, h])

    barrier = pltpu.get_barrier_semaphore()
    for s in range(1, NT):
        pl.semaphore_signal(barrier, inc=1, device_id={"tm": zpeer(s)}, device_id_type=MESH)
    pl.semaphore_signal(barrier, inc=1, device_id=partner, device_id_type=MESH)
    for k in range(1, NS):
        pl.semaphore_signal(barrier, inc=1, device_id={"space": lax.rem(sp + k, NS)}, device_id_type=MESH)

    for s in range(NT):
        for h in range(2):
            field_copy(s, h).start()

    l32 = l_ref[...].astype(F32)
    t32 = t_ref[...].astype(F32)
    l32t, t32t = l32.T, t32.T
    for k in range(nk):
        khat[pl.ds(k * nj, nj), :] = (l32 * t32[k:k + 1, :]).astype(BF16)
        khat_t[:, pl.ds(k * nj, nj)] = (l32t * t32t[:, k:k + 1]).astype(BF16)
    ag[0, pl.ds(0, 128), :] = s_ref[...]
    proj[...] = jnp.zeros_like(proj)
    sq[...] = jnp.zeros_like(sq)

    pl.semaphore_wait(barrier, NT - 1 + 1 + NS - 1)

    def ag_z(s):
        m = mirror(s)
        return remote(s_ref, ag.at[m, pl.ds(0, 128)], agz_s.at[s], agz_r.at[m], {"tm": zpeer(s)})

    def ag_z_in(s):
        return remote(s_ref, ag.at[s, pl.ds(0, 128)], agz_s.at[s], agz_r.at[s], {"tm": zpeer(s)})

    def ag_x(s):
        src = s_ref if isinstance(s, int) and s == 0 else ag.at[s, pl.ds(0, 128)]
        return remote(src, ag.at[s, pl.ds(128, 128)], agx_s.at[s], agx_r.at[s], partner)

    ag_x(0).start()
    for s in range(1, NT):
        ag_z(s).start()
    for s in range(1, NT):
        ag_z_in(s).wait_recv()
        ag_x(s).start()

    def rs_x(s):
        return remote(part.at[s, 1], xbuf.at[s], rx_s.at[s], rx_r.at[s], partner)

    def step(s, carry):
        for h in range(2):
            field_copy(s, h).wait()
        ag_x_in = remote(s_ref, ag.at[s, pl.ds(128, 128)], agx_s.at[s], agx_r.at[s], partner)
        ag_x_in.wait_recv()
        sb = ag[s]
        per = CHUNK // nj
        for c in range(nk // per):
            rows = pl.ds(c * CHUNK, CHUNK)
            model = lax.dot_general(khat[rows, :], sb, (((1,), (1,)), ((), ())), preferred_element_type=F32)
            data = fbuf[s, pl.ds(c * per, per), :, :].reshape(CHUNK, 256).astype(F32)
            misfit = model - data
            sq[...] += jnp.sum((misfit * misfit).reshape(CHUNK // 8, 8, 256), axis=0)
            mb[rows, :] = misfit.astype(BF16)
        grad = jnp.dot(khat_t[...], mb[...], preferred_element_type=F32)
        part[s, 0] = grad[:, :128]
        part[s, 1] = grad[:, 128:]
        rs_x(s).start()
        proj[...] += jnp.dot(mb[...], sb, preferred_element_type=F32)
        return carry

    lax.fori_loop(0, NT, step, 0)

    glf[...] = jnp.zeros_like(glf)
    gts = []
    for k in range(nk):
        pk = proj[pl.ds(k * nj, nj), :]
        glf[...] += pk * t32[k:k + 1, :]
        gts.append(jnp.sum(pk * l32, axis=0, keepdims=True))
    gt_part = jnp.concatenate(gts, axis=0)
    loss_part = sq[:, :128] + sq[:, 128:]
    for q in range(NS):
        m1[q, pl.ds(0, 8), :] = glf[pl.ds(q * 8, 8), :]
        m1[q, pl.ds(8, 16), :] = gt_part
        m1[q, pl.ds(24, 8), :] = loss_part

    def plane(k):
        return lax.rem(sp + k, NS)

    def p1(k):
        q = plane(k)
        return remote(m1.at[q], r1.at[sp], p1_s.at[k], p1_r.at[sp], {"space": q})

    def p1_in(k):
        q = plane(k)
        return remote(m1.at[q], r1.at[q], p1_s.at[k], p1_r.at[q], {"space": q})

    for k in range(1, NS):
        p1(k).start()
    r1[sp] = m1[sp]

    def rs_z(s):
        m = mirror(s)
        return remote(zs.at[s], zbuf.at[m], rz_s.at[s], rz_r.at[m], {"tm": zpeer(s)})

    def rs_z_in(s):
        return remote(zs.at[s], zbuf.at[s], rz_s.at[s], rz_r.at[s], {"tm": zpeer(s)})

    for s in (1, 2, 3, 4, 5, 6, 7):
        rs_x(s).wait_recv()
        zs[s] = part[s, 0] + xbuf[s]
        rs_z(s).start()
    rs_x(0).wait_recv()

    for k in range(1, NS):
        p1_in(k).wait_recv()
    plane_sum = r1[0]
    for q in range(1, NS):
        plane_sum = plane_sum + r1[q]
    m2[pl.ds(0, 8), :] = plane_sum[0:8, :]
    m2[pl.ds(8, 8), :] = plane_sum[24:32, :]
    m3[pl.ds(0, 16), :] = plane_sum[8:24, :]

    def p2(s):
        return remote(m2, r2.at[t], p2_s.at[s], p2_r.at[t], {"tm": zpeer(s)})

    def p2_in(s):
        return remote(m2, r2.at[zpeer(s)], p2_s.at[s], p2_r.at[zpeer(s)], {"tm": zpeer(s)})

    for s in range(1, NT):
        p2(s).start()
    r2[t] = m2[...]
    for s in range(1, NT):
        p2_in(s).wait_recv()
    tm_sum = r2[0]
    for q in range(1, NT):
        tm_sum = tm_sum + r2[q]
    m3[pl.ds(16, 8), :] = tm_sum[8:16, :]
    px = remote(m3, r3, px_s, px_r, partner)
    px.start()
    glf[pl.ds(pl.multiple_of(sp * 8, 8), 8), :] = tm_sum[0:8, :] * scales[1]

    def p3(k):
        rows = pl.ds(pl.multiple_of(sp * 8, 8), 8)
        return remote(glf.at[rows], glf.at[rows], p3_s.at[k], p3_r.at[sp], {"space": plane(k)})

    def p3_in(k):
        rows = pl.ds(pl.multiple_of(plane(k) * 8, 8), 8)
        return remote(glf.at[rows], glf.at[rows], p3_s.at[k], p3_r.at[plane(k)], {"space": plane(k)})

    for k in range(1, NS):
        p3(k).start()

    total = part[0, 0] + xbuf[0]
    for s in range(1, NT):
        rs_z_in(s).wait_recv()
        total = total + zbuf[s]
    gs_ref[...] = total.T * scales[0]

    px.wait_recv()
    both = m3[...] + r3[...]
    gt_ref[...] = both[0:16, :] * scales[2]
    loss_ref[0, 0] = jnp.sum(both[16:24, :]) * scales[3]
    for k in range(1, NS):
        p3_in(k).wait_recv()
    gl_ref[...] = glf[...]

    px.wait_send()
    for s in range(NT):
        remote(s_ref, ag.at[s, pl.ds(128, 128)], agx_s.at[s], agx_r.at[s], partner).wait_send()
        rs_x(s).wait_send()
    for s in range(1, NT):
        ag_z(s).wait_send()
        rs_z(s).wait_send()
        p2(s).wait_send()
    for k in range(1, NS):
        p1(k).wait_send()
        p3(k).wait_send()


def on_device(field, factor_space, factor_level, factor_time):
    nk, nj, ni = field.shape
    own = factor_space.shape[0]
    kj = nk * nj
    count_i, count_j, count_k = own * NS * NV * NT, nj * NV, nk * NT
    scales = (
        1.0 / (count_j * count_k) ** 0.5,
        1.0 / (count_i * count_k) ** 0.5,
        1.0 / (count_i * count_j) ** 0.5,
        0.5 / (count_i * count_j * count_k),
    )
    dma = pltpu.SemaphoreType.DMA
    vmem = pl.BlockSpec(memory_space=pltpu.VMEM)
    gs, gl, gt, loss = pl.pallas_call(
        functools.partial(kernel, scales),
        out_shape=(
            jax.ShapeDtypeStruct((own, 128), F32),
            jax.ShapeDtypeStruct((nj, 128), F32),
            jax.ShapeDtypeStruct((nk, 128), F32),
            jax.ShapeDtypeStruct((1, 1), F32),
        ),
        in_specs=[pl.BlockSpec(memory_space=pl.ANY), vmem, vmem, vmem],
        out_specs=(vmem, vmem, vmem, pl.BlockSpec(memory_space=pltpu.SMEM)),
        scratch_shapes=[
            pltpu.VMEM((NT, nk, nj, 256), BF16),
            pltpu.VMEM((NT, 256, 128), BF16),
            pltpu.VMEM((kj, 128), BF16),
            pltpu.VMEM((128, kj), BF16),
            pltpu.VMEM((kj, 256), BF16),
            pltpu.VMEM((kj, 128), F32),
            pltpu.VMEM((8, 256), F32),
            pltpu.VMEM((NT, 2, 128, 128), F32),
            pltpu.VMEM((NT, 128, 128), F32),
            pltpu.VMEM((NT, 128, 128), F32),
            pltpu.VMEM((NT, 128, 128), F32),
            pltpu.VMEM((NS, 32, 128), F32),
            pltpu.VMEM((NS, 32, 128), F32),
            pltpu.VMEM((16, 128), F32),
            pltpu.VMEM((NT, 16, 128), F32),
            pltpu.VMEM((24, 128), F32),
            pltpu.VMEM((24, 128), F32),
            pltpu.VMEM((nj, 128), F32),
            dma((NT, 2)),
            dma((NT,)), dma((NT,)), dma((NT,)), dma((NT,)),
            dma((NT,)), dma((NT,)), dma((NT,)), dma((NT,)),
            dma((NS,)), dma((NS,)), dma((NT,)), dma((NT,)), dma((NS,)), dma((NS,)),
            dma, dma,
        ],
        compiler_params=pltpu.CompilerParams(collective_id=0, has_side_effects=True,
                                             vmem_limit_bytes=40 * 2**20),
    )(field, factor_space, factor_level, factor_time)
    return gs, gl, gt, loss.reshape(())


def solution(mesh):
    placed = (
        P("tm", "var", "space"),
        P(("space", "var", "tm"), None),
        P("var", None),
        P("tm", None),
    )
    return jax.shard_map(
        on_device,
        mesh=mesh,
        in_specs=placed,
        out_specs=(P(("space", "var", "tm"), None), P("var", None), P("tm", None), P()),
        check_vma=False,
    )
```

```python
import functools

import jax
import jax.numpy as jnp
from jax import lax
from jax.experimental import pallas as pl
from jax.experimental.pallas import tpu as pltpu
from jax.sharding import PartitionSpec as P

MESH = pl.DeviceIdType.MESH
BF16, F32 = jnp.bfloat16, jnp.float32
NS, NV, NT = 16, 2, 8
NA, NX = 8, 2
NB = NX * NT
CHUNK = 512


def offset_of(s):
    if isinstance(s, int):
        return (0, 4, 3, 5, 2, 6, 1, 7)[s]
    mag = NT // 2 - s // 2
    signed = jnp.where(s % 2 == 0, mag, NT - mag)
    return jnp.where(s == 0, 0, jnp.where(s == 1, NT // 2, signed))


def mirror(s):
    return (0, 1, 3, 2, 5, 4, 7, 6)[s]


def kernel(scales, field, s_hbm, l_hbm, t_hbm, gs_ref, gl_ref, gt_ref, loss_ref,
           s_ref, l_ref, t_ref, fbuf, ag, khat, khat_t, mb, proj, sq, part, xbuf, zs, zbuf, rbuf, tbuf, hbuf,
           glf, r1, g1, q1, m2, r2, g2, q2, m3, r3, glo,
           isem, fsem, agz_s, agz_r, agx_s, agx_r, rx_s, rx_r, rz_s, rz_r, rr_s, rr_r, rh_s, rh_r,
           a1_s, a1_r, b1_s, b1_r, a2_s, a2_r, b2_s, b2_r, a3_s, a3_r, b3_s, b3_r):
    sp, v, t = lax.axis_index("space"), lax.axis_index("var"), lax.axis_index("tm")
    xh, a = sp // NA, sp % NA
    xc = xh * NV + v
    b = xh * NT + t
    partner = {"var": 1 - v}
    nk, nj = t_ref.shape[0], l_ref.shape[0]

    def zpeer(s):
        return lax.rem(t + offset_of(s), NT)

    def apeer(k):
        return lax.rem(a + k, NA)

    def a_id(k):
        return {"space": xh * NA + apeer(k)}

    def bpeer(k):
        return lax.rem(xh + k // NT, NX) * NT + lax.rem(t + k, NT)

    def b_id(k):
        return {"space": lax.rem(xh + k // NT, NX) * NA + a, "tm": lax.rem(t + k, NT)}

    def xpeer(k):
        return lax.rem(xc + k, NX * NV)

    def x_id(k):
        return {"space": xpeer(k) // NV * NA + a, "var": xpeer(k) % NV}

    def remote(src, dst, send, recv, dev):
        return pltpu.make_async_remote_copy(src_ref=src, dst_ref=dst, send_sem=send, recv_sem=recv,
                                            device_id=dev, device_id_type=MESH)

    small = [pltpu.make_async_copy(x, y, isem.at[i])
             for i, (x, y) in enumerate(((l_hbm, l_ref), (t_hbm, t_ref), (s_hbm, s_ref)))]
    for copy in small:
        copy.start()

    barrier = pltpu.get_barrier_semaphore()
    for k in range(1, NB):
        pl.semaphore_signal(barrier, inc=1, device_id=b_id(k), device_id_type=MESH)
    pl.semaphore_signal(barrier, inc=1, device_id=partner, device_id_type=MESH)
    pl.semaphore_signal(barrier, inc=1, device_id={"space": (1 - xh) * NA + a, "var": 1 - v}, device_id_type=MESH)
    for k in range(1, NA):
        pl.semaphore_signal(barrier, inc=1, device_id=a_id(k), device_id_type=MESH)

    def turn_of(i):
        if isinstance(i, int):
            return ((0, 0), (0, 1), (1, 0), (0, 2), (1, 1), (0, 3), (1, 2), (1, 3))[i]
        w = jnp.where(i == 7, 1, jnp.where(i == 0, 0, 1 - i % 2))
        return w, jnp.where(w == 1, (i - 1) // 2, (i + 1) // 2)

    def field_copy(i, h):
        w, p = turn_of(i)
        own = v + w * (1 - 2 * v)
        owner = own * NT + lax.rem(t + offset_of(2 * p + h), NT)
        cols = pl.ds(pl.multiple_of(owner * 128, 128), 128)
        return pltpu.make_async_copy(field.at[:, :, cols], fbuf.at[i, :, :, pl.ds(h * 128, 128)], fsem.at[i, h])

    for i in range(NT):
        for h in range(2):
            field_copy(i, h).start()

    for copy in small:
        copy.wait()
    l32 = l_ref[...].astype(F32)
    t32 = t_ref[...].astype(F32)
    l32t, t32t = l32.T, t32.T
    for k in range(nk):
        khat[pl.ds(k * nj, nj), :] = (l32 * t32[k:k + 1, :]).astype(BF16)
        khat_t[:, pl.ds(k * nj, nj)] = (l32t * t32t[:, k:k + 1]).astype(BF16)
    ag[0, 0, pl.ds(0, 128), :] = s_ref[...]
    proj[...] = jnp.zeros_like(proj)
    sq[...] = jnp.zeros_like(sq)

    pl.semaphore_wait(barrier, NB - 1 + 2 + NA - 1)

    def slot(w, s):
        return ag.at[w, s // 2, pl.ds((s % 2) * 128, 128)]

    def ag_z(s):
        return remote(s_ref, slot(0, mirror(s)), agz_s.at[s], agz_r.at[mirror(s)], {"tm": zpeer(s)})

    def ag_z_in(s):
        return remote(s_ref, slot(0, s), agz_s.at[s], agz_r.at[s], {"tm": zpeer(s)})

    def ag_x(p, h):
        rows = pl.ds(h * 128, 128)
        return remote(ag.at[0, p, rows], ag.at[1, p, rows], agx_s.at[p, h], agx_r.at[p, h], partner)

    remote(s_ref, slot(1, 0), agx_s.at[0, 0], agx_r.at[0, 0], partner).start()
    for s in range(1, NT):
        ag_z(s).start()

    def pass_on(p, h):
        s = 2 * p + h
        rows = pl.ds(h * 128, 128)
        remote(s_ref, ag.at[0, p, rows], agz_s.at[s], agz_r.at[s], partner).wait_recv()
        ag_x(p, h).start()

    def rs_x(p):
        two = pl.ds(2 * p, 2)
        return remote(part.at[1, two], xbuf.at[two], rx_s.at[p], rx_r.at[p], partner)

    rs_x1 = remote(part.at[1, 1], xbuf.at[1], rx_s.at[0], rx_r.at[0], partner)
    rs_x0 = remote(zs.at[0], xbuf.at[0], rx_s.at[3], rx_r.at[3], partner)

    def z_to(k):
        return {"tm": lax.rem(t + k, NT)}

    def near(s):
        m = mirror(s)
        return remote(part.at[0, s], zbuf.at[m], rz_s.at[s], rz_r.at[m], z_to(offset_of(s)))

    def relay(s):
        return remote(part.at[1, s], rbuf.at[s - 6], rr_s.at[s - 6], rr_r.at[s - 6], z_to(offset_of(s)))

    def half(h):
        rows = pl.ds(64 * h, 64)
        return remote(zs.at[1, rows], hbuf.at[h], rh_s.at[h], rh_r.at[h], z_to((2, 6)[h]))

    def short(s):
        return remote(zs.at[s], tbuf.at[s - 2], rz_s.at[s], rz_r.at[s], z_to((1, 7)[s - 2]))

    def last(s):
        m = mirror(s)
        return remote(zs.at[s], zbuf.at[m], rz_s.at[s], rz_r.at[m], z_to(offset_of(s)))

    def turn(i, carry):
        w, p = turn_of(i)

        @pl.when((i == 1) | (i == 3) | (i == 4))
        def _():
            for h in range(2):
                pass_on(jnp.where(i == 1, 1, i - 1), h)

        @pl.when(i == 7)
        def _():
            rs_x1.wait_recv()
            zs[1] = part[0, 1] + xbuf[1]
            for h in range(2):
                half(h).start()

        for h in range(2):
            field_copy(i, h).wait()

        @pl.when(w == 1)
        def _():
            for h in range(2):
                ag_x(p, h).wait_recv()

        sb = ag[w, p]
        per = CHUNK // nj
        acc = sq[...]
        for c in range(nk // per):
            rows = pl.ds(c * CHUNK, CHUNK)
            model = lax.dot_general(khat[rows, :], sb, (((1,), (1,)), ((), ())), preferred_element_type=F32)
            data = fbuf[i, pl.ds(c * per, per), :, :].reshape(CHUNK, 256).astype(F32)
            misfit = model - data
            acc = acc + jnp.sum((misfit * misfit).reshape(CHUNK // 8, 8, 256), axis=0)
            mb[rows, :] = misfit.astype(BF16)
        sq[...] = acc
        grad = jnp.dot(khat_t[...], mb[...], preferred_element_type=F32)
        part[w, 2 * p] = grad[:, :128]
        part[w, 2 * p + 1] = grad[:, 128:]

        @pl.when(i == 2)
        def _():
            rs_x1.start()

        @pl.when((i == 4) | (i == 6))
        def _():
            rs_x(p).start()

        @pl.when(i == 5)
        def _():
            for s in (6, 7):
                near(s).start()

        @pl.when(i == 7)
        def _():
            for s in (6, 7):
                relay(s).start()

        proj[...] += jnp.dot(mb[...], sb, preferred_element_type=F32)
        return carry

    pass_on(0, 1)
    lax.fori_loop(0, NT, turn, 0)

    ra = nj // NA

    def a_rows(q):
        return pl.ds(pl.multiple_of(q * ra, ra), ra)

    def level_rows(q):
        total = jnp.zeros((ra, 128), F32)
        for k in range(nk):
            rows = pl.ds(pl.multiple_of(k * nj + q * ra, ra), ra)
            total = total + proj[rows, :] * t32[k:k + 1, :]
        return total

    def a1(k):
        return remote(glf.at[apeer(k)], r1.at[a], a1_s.at[k], a1_r.at[a], a_id(k))

    def a1_in(k):
        return remote(glf.at[apeer(k)], r1.at[apeer(k)], a1_s.at[k], a1_r.at[apeer(k)], a_id(k))

    for k in range(1, NA):
        glf[apeer(k)] = level_rows(apeer(k))
        a1(k).start()
    r1[a] = level_rows(a)

    for k in range(nk):
        g1[pl.ds(k, 1), :] = jnp.sum(proj[pl.ds(k * nj, nj), :] * l32, axis=0, keepdims=True)
    g1[pl.ds(nk, 8), :] = sq[:, :128] + sq[:, 128:]

    def b1(k):
        return remote(g1, q1.at[a], b1_s.at[k], b1_r.at[a], a_id(k))

    def b1_in(k):
        return remote(g1, q1.at[apeer(k)], b1_s.at[k], b1_r.at[apeer(k)], a_id(k))

    for k in range(1, NA):
        b1(k).start()
    q1[a] = g1[...]

    rs_x(1).wait_recv()
    for s in (2, 3):
        zs[s] = part[0, s] + xbuf[s]
        short(s).start()

    for k in range(1, NA):
        a1_in(k).wait_recv()
    total = r1[0]
    for q in range(1, NA):
        total = total + r1[q]
    m2[...] = total

    def a2(k):
        return remote(m2, r2.at[b], a2_s.at[k], a2_r.at[b], b_id(k))

    def a2_in(k):
        return remote(m2, r2.at[bpeer(k)], a2_s.at[k], a2_r.at[bpeer(k)], b_id(k))

    for k in range(1, NB):
        a2(k).start()
    r2[b] = m2[...]

    for k in range(1, NA):
        b1_in(k).wait_recv()
    total = q1[0]
    for q in range(1, NA):
        total = total + q1[q]
    g2[...] = total

    def b2(k):
        return remote(g2, q2.at[xc], b2_s.at[k], b2_r.at[xc], x_id(k))

    def b2_in(k):
        return remote(g2, q2.at[xpeer(k)], b2_s.at[k], b2_r.at[xpeer(k)], x_id(k))

    for k in range(1, NX * NV):
        b2(k).start()
    q2[xc] = g2[...]

    for s in (6, 7):
        relay(s).wait_recv()
    zs[0] = part[1, 0] + rbuf[0] + rbuf[1]
    rs_x0.start()

    rs_x(2).wait_recv()
    for s in (4, 5):
        h = s - 4
        short(s - 2).wait_recv()
        half(h).wait_recv()
        zs[s] = part[0, s] + xbuf[s] + tbuf[h]
        rows = pl.ds(64 * h, 64)
        zs[s, rows] += hbuf[h]
        last(s).start()

    for k in range(1, NX * NV):
        b2_in(k).wait_recv()
    total = q2[0]
    for q in range(1, NX * NV):
        total = total + q2[q]
    gt_ref[...] = total[0:nk, :] * scales[2]
    m3[...] = total[nk:nk + 8, :]

    def b3(s):
        return remote(m3, r3.at[t], b3_s.at[s], b3_r.at[t], {"tm": zpeer(s)})

    def b3_in(s):
        return remote(m3, r3.at[zpeer(s)], b3_s.at[s], b3_r.at[zpeer(s)], {"tm": zpeer(s)})

    for s in range(1, NT):
        b3(s).start()
    r3[t] = m3[...]

    for k in range(1, NB):
        a2_in(k).wait_recv()
    total = r2[0]
    for q in range(1, NB):
        total = total + r2[q]
    glo[a_rows(a), :] = total * scales[1]

    def a3(k):
        return remote(glo.at[a_rows(a)], glo.at[a_rows(a)], a3_s.at[k], a3_r.at[a], a_id(k))

    def a3_in(k):
        rows = a_rows(apeer(k))
        return remote(glo.at[rows], glo.at[rows], a3_s.at[k], a3_r.at[apeer(k)], a_id(k))

    for k in range(1, NA):
        a3(k).start()

    rs_x0.wait_recv()
    total = part[0, 0] + xbuf[0]
    for s in (6, 7, 4, 5):
        remote(zs.at[s], zbuf.at[s], rz_s.at[s], rz_r.at[s], partner).wait_recv()
        total = total + zbuf[s]
    gs_ref[...] = total.T * scales[0]

    for s in range(1, NT):
        b3_in(s).wait_recv()
    total = r3[0]
    for q in range(1, NT):
        total = total + r3[q]
    loss_ref[0, 0] = jnp.sum(total) * scales[3]
    for k in range(1, NA):
        a3_in(k).wait_recv()
    gl_ref[...] = glo[...]

    rs_x0.wait_send()
    rs_x1.wait_send()
    for p in (1, 2):
        rs_x(p).wait_send()
    for h in range(2):
        half(h).wait_send()
        short(2 + h).wait_send()
        last(4 + h).wait_send()
        near(6 + h).wait_send()
        relay(6 + h).wait_send()
    for p in range(NT // 2):
        for h in range(2):
            ag_x(p, h).wait_send()
    for s in range(1, NT):
        ag_z(s).wait_send()
        b3(s).wait_send()
    for k in range(1, NA):
        a1(k).wait_send()
        b1(k).wait_send()
        a3(k).wait_send()
    for k in range(1, NB):
        a2(k).wait_send()
    for k in range(1, NX * NV):
        b2(k).wait_send()


def on_device(field, factor_space, factor_level, factor_time):
    nk, nj, ni = field.shape
    own = factor_space.shape[0]
    kj = nk * nj
    count_i, count_j, count_k = own * NS * NV * NT, nj * NV, nk * NT
    scales = (
        1.0 / (count_j * count_k) ** 0.5,
        1.0 / (count_i * count_k) ** 0.5,
        1.0 / (count_i * count_j) ** 0.5,
        0.5 / (count_i * count_j * count_k),
    )
    dma = pltpu.SemaphoreType.DMA
    vmem = pl.BlockSpec(memory_space=pltpu.VMEM)
    inputs = [pltpu.with_memory_space_constraint(x, pltpu.HBM)
              for x in (field, factor_space, factor_level, factor_time)]
    gs, gl, gt, loss = pl.pallas_call(
        functools.partial(kernel, scales),
        out_shape=(
            jax.ShapeDtypeStruct((own, 128), F32),
            jax.ShapeDtypeStruct((nj, 128), F32),
            jax.ShapeDtypeStruct((nk, 128), F32),
            jax.ShapeDtypeStruct((1, 1), F32),
        ),
        in_specs=[pl.BlockSpec(memory_space=pltpu.HBM)] * 4,
        out_specs=(vmem, vmem, vmem, pl.BlockSpec(memory_space=pltpu.SMEM)),
        scratch_shapes=[
            pltpu.VMEM((own, 128), BF16),
            pltpu.VMEM((nj, 128), BF16),
            pltpu.VMEM((nk, 128), BF16),
            pltpu.VMEM((NT, nk, nj, 256), BF16),
            pltpu.VMEM((NV, NT // 2, 256, 128), BF16),
            pltpu.VMEM((kj, 128), BF16),
            pltpu.VMEM((128, kj), BF16),
            pltpu.VMEM((kj, 256), BF16),
            pltpu.VMEM((kj, 128), F32),
            pltpu.VMEM((8, 256), F32),
            pltpu.VMEM((NV, NT, 128, 128), F32),
            pltpu.VMEM((NT, 128, 128), F32),
            pltpu.VMEM((NT, 128, 128), F32),
            pltpu.VMEM((NT, 128, 128), F32),
            pltpu.VMEM((2, 128, 128), F32),
            pltpu.VMEM((2, 128, 128), F32),
            pltpu.VMEM((2, 64, 128), F32),
            pltpu.VMEM((NA, nj // NA, 128), F32),
            pltpu.VMEM((NA, nj // NA, 128), F32),
            pltpu.VMEM((nk + 8, 128), F32),
            pltpu.VMEM((NA, nk + 8, 128), F32),
            pltpu.VMEM((nj // NA, 128), F32),
            pltpu.VMEM((NB, nj // NA, 128), F32),
            pltpu.VMEM((nk + 8, 128), F32),
            pltpu.VMEM((NX * NV, nk + 8, 128), F32),
            pltpu.VMEM((8, 128), F32),
            pltpu.VMEM((NT, 8, 128), F32),
            pltpu.VMEM((nj, 128), F32),
            dma((3,)), dma((NT, 2)),
            dma((NT,)), dma((NT,)), dma((NT // 2, 2)), dma((NT // 2, 2)),
            dma((NT // 2,)), dma((NT // 2,)), dma((NT,)), dma((NT,)),
            dma((2,)), dma((2,)), dma((2,)), dma((2,)),
            dma((NA,)), dma((NA,)), dma((NA,)), dma((NA,)),
            dma((NB,)), dma((NB,)), dma((NX * NV,)), dma((NX * NV,)),
            dma((NA,)), dma((NA,)), dma((NT,)), dma((NT,)),
        ],
        compiler_params=pltpu.CompilerParams(collective_id=0, has_side_effects=True,
                                             vmem_limit_bytes=40 * 2**20),
    )(*inputs)
    return gs, gl, gt, loss.reshape(())


def solution(mesh):
    placed = (
        P("tm", "var", "space"),
        P(("space", "var", "tm"), None),
        P("var", None),
        P("tm", None),
    )
    return jax.shard_map(
        on_device,
        mesh=mesh,
        in_specs=placed,
        out_specs=(P(("space", "var", "tm"), None), P("var", None), P("tm", None), P()),
        check_vma=False,
    )
```

```python
import functools

import jax
import jax.numpy as jnp
from jax import lax
from jax.experimental import pallas as pl
from jax.experimental.pallas import tpu as pltpu
from jax.sharding import PartitionSpec as P

MESH = pl.DeviceIdType.MESH
BF16, F32 = jnp.bfloat16, jnp.float32
NS, NV, NT = 16, 2, 8
NA, NX = 8, 2
CHUNK = 512


def offset_of(s):
    if isinstance(s, int):
        return (0, 4, 3, 5, 2, 6, 1, 7)[s]
    mag = NT // 2 - s // 2
    signed = jnp.where(s % 2 == 0, mag, NT - mag)
    return jnp.where(s == 0, 0, jnp.where(s == 1, NT // 2, signed))


def mirror(s):
    return (0, 1, 3, 2, 5, 4, 7, 6)[s]


def kernel(scales, field, s_hbm, l_hbm, t_hbm, gs_ref, gl_ref, gt_ref, loss_ref,
           s_ref, l_ref, t_ref, fbuf, ag, khat, khat_t, mb, proj, sq, part, xbuf, zs, zbuf, rbuf, tbuf, hbuf,
           glf, r1, g1, q1, m2, r2, g2, q2, m3, r3, glo,
           isem, fsem, agh_s, agh_r, agz_s, agz_r, agx_s, agx_r, rx_s, rx_r, rz_s, rz_r, rr_s, rr_r, rh_s, rh_r,
           a1_s, a1_r, b1_s, b1_r, a2_s, a2_r, b2_s, b2_r, a3_s, a3_r, b3_s, b3_r):
    sp, v, t = lax.axis_index("space"), lax.axis_index("var"), lax.axis_index("tm")
    xh, a = sp // NA, sp % NA
    xc = xh * NV + v
    partner = {"var": 1 - v}
    nk, nj = t_ref.shape[0], l_ref.shape[0]

    def zpeer(s):
        return lax.rem(t + offset_of(s), NT)

    def apeer(k):
        return lax.rem(a + k, NA)

    def a_id(k):
        return {"space": xh * NA + apeer(k)}

    def ppeer(k):
        return lax.rem(sp + k, NS)

    def p_id(k):
        return {"space": ppeer(k)}

    def xpeer(k):
        return lax.rem(xc + k, NX * NV)

    def x_id(k):
        return {"space": xpeer(k) // NV * NA + a, "var": xpeer(k) % NV}

    def remote(src, dst, send, recv, dev):
        return pltpu.make_async_remote_copy(src_ref=src, dst_ref=dst, send_sem=send, recv_sem=recv,
                                            device_id=dev, device_id_type=MESH)

    small = [pltpu.make_async_copy(x, y, isem.at[i])
             for i, (x, y) in enumerate(((l_hbm, l_ref), (t_hbm, t_ref), (s_hbm, s_ref)))]
    for copy in small:
        copy.start()

    barrier = pltpu.get_barrier_semaphore()
    for s in range(1, NT):
        pl.semaphore_signal(barrier, inc=1, device_id={"tm": zpeer(s)}, device_id_type=MESH)
    pl.semaphore_signal(barrier, inc=1, device_id=partner, device_id_type=MESH)
    pl.semaphore_signal(barrier, inc=1, device_id={"space": (1 - xh) * NA + a, "var": 1 - v}, device_id_type=MESH)
    for k in range(1, NS):
        pl.semaphore_signal(barrier, inc=1, device_id=p_id(k), device_id_type=MESH)

    def turn_of(i):
        if isinstance(i, int):
            return ((0, 2), (0, 1), (1, 2), (0, 3), (0, 0), (1, 1), (1, 3), (1, 0))[i]
        w = jnp.where((i == 2) | (i >= 5), 1, 0)
        p = jnp.where((i == 3) | (i == 6), 3, 0)
        p = jnp.where((i == 1) | (i == 5), 1, p)
        return w, jnp.where((i == 0) | (i == 2), 2, p)

    def field_copy(i, h):
        w, p = turn_of(i)
        own = v + w * (1 - 2 * v)
        owner = own * NT + lax.rem(t + offset_of(2 * p + h), NT)
        cols = pl.ds(pl.multiple_of(owner * 128, 128), 128)
        return pltpu.make_async_copy(field.at[:, :, cols], fbuf.at[i, :, :, pl.ds(h * 128, 128)], fsem.at[i, h])

    for i in range(NT):
        for h in range(2):
            field_copy(i, h).start()

    for copy in small:
        copy.wait()
    l32 = l_ref[...].astype(F32)
    t32 = t_ref[...].astype(F32)
    l32t, t32t = l32.T, t32.T
    for k in range(nk):
        khat[pl.ds(k * nj, nj), :] = (l32 * t32[k:k + 1, :]).astype(BF16)
        khat_t[:, pl.ds(k * nj, nj)] = (l32t * t32t[:, k:k + 1]).astype(BF16)
    ag[0, 0, pl.ds(0, 128), :] = s_ref[...]
    proj[...] = jnp.zeros_like(proj)
    sq[...] = jnp.zeros_like(sq)

    pl.semaphore_wait(barrier, NT - 1 + 2 + NS - 1)

    def slot(w, s):
        return ag.at[w, s // 2, pl.ds((s % 2) * 128, 128)]

    def ag_z(s):
        return remote(s_ref, slot(0, mirror(s)), agz_s.at[s], agz_r.at[mirror(s)], {"tm": zpeer(s)})

    def ag_z_in(s):
        return remote(s_ref, slot(0, s), agz_s.at[s], agz_r.at[s], {"tm": zpeer(s)})

    def ag_x(p, h):
        rows = pl.ds(h * 128, 128)
        return remote(ag.at[0, p, rows], ag.at[1, p, rows], agx_s.at[p, h], agx_r.at[p, h], partner)

    remote(s_ref, slot(1, 0), agx_s.at[0, 0], agx_r.at[0, 0], partner).start()
    for s in (4, 5, 2, 3, 6, 7):
        ag_z(s).start()

    def ag_half(h):
        return remote(ag.at[0, 2, pl.ds(128 * h + 64 * h, 64)], ag.at[0, 0, pl.ds(128 + 64 * h, 64)],
                      agh_s.at[h], agh_r.at[h], {"tm": lax.rem(t + (6, 2)[h], NT)})

    def pass_on(p, h):
        s = 2 * p + h
        rows = pl.ds(h * 128, 128)
        remote(s_ref, ag.at[0, p, rows], agz_s.at[s], agz_r.at[s], partner).wait_recv()
        ag_x(p, h).start()

    def rs_x(p):
        two = pl.ds(2 * p, 2)
        return remote(part.at[1, two], xbuf.at[two], rx_s.at[p], rx_r.at[p], partner)

    rs_x1 = remote(part.at[1, 1], xbuf.at[1], rx_s.at[0], rx_r.at[0], partner)
    rs_x0 = remote(zs.at[0], xbuf.at[0], rx_s.at[3], rx_r.at[3], partner)

    def z_to(k):
        return {"tm": lax.rem(t + k, NT)}

    def near(s):
        m = mirror(s)
        return remote(part.at[0, s], zbuf.at[m], rz_s.at[s], rz_r.at[m], z_to(offset_of(s)))

    def relay(s):
        return remote(part.at[1, s], rbuf.at[s - 6], rr_s.at[s - 6], rr_r.at[s - 6], z_to(offset_of(s)))

    def half(h):
        rows = pl.ds(64 * h, 64)
        return remote(zs.at[1, rows], hbuf.at[h], rh_s.at[h], rh_r.at[h], z_to((2, 6)[h]))

    def short(s):
        return remote(zs.at[s], tbuf.at[s - 2], rz_s.at[s], rz_r.at[s], z_to((1, 7)[s - 2]))

    def last(s):
        m = mirror(s)
        return remote(zs.at[s], zbuf.at[m], rz_s.at[s], rz_r.at[m], z_to(offset_of(s)))

    def turn(i, carry):
        w, p = turn_of(i)

        @pl.when((i == 1) | (i == 3))
        def _():
            for h in range(2):
                pass_on(i, h)

        @pl.when(i == 4)
        def _():
            for h in range(2):
                ag_half(h).wait_recv()
            ag_x(0, 1).start()

        for h in range(2):
            field_copy(i, h).wait()

        @pl.when(w == 1)
        def _():
            for h in range(2):
                ag_x(p, h).wait_recv()

        sb = ag[w, p]
        per = CHUNK // nj
        acc = sq[...]
        for c in range(nk // per):
            rows = pl.ds(c * CHUNK, CHUNK)
            model = lax.dot_general(khat[rows, :], sb, (((1,), (1,)), ((), ())), preferred_element_type=F32)
            data = fbuf[i, pl.ds(c * per, per), :, :].reshape(CHUNK, 256).astype(F32)
            misfit = model - data
            acc = acc + jnp.sum((misfit * misfit).reshape(CHUNK // 8, 8, 256), axis=0)
            mb[rows, :] = misfit.astype(BF16)
        sq[...] = acc
        grad = jnp.dot(khat_t[...], mb[...], preferred_element_type=F32)
        part[w, 2 * p] = grad[:, :128]
        part[w, 2 * p + 1] = grad[:, 128:]

        @pl.when((i == 2) | (i == 5))
        def _():
            rs_x(p).start()

        @pl.when(i == 3)
        def _():
            for s in (6, 7):
                near(s).start()

        @pl.when(i == 6)
        def _():
            for s in (6, 7):
                relay(s).start()

        @pl.when(i == 7)
        def _():
            rs_x1.start()

        proj[...] += jnp.dot(mb[...], sb, preferred_element_type=F32)
        return carry

    for h in range(2):
        ag_z_in(4 + h).wait_recv()
        ag_half(h).start()
        ag_x(2, h).start()
    lax.fori_loop(0, NT, turn, 0)

    ra = nj // NS

    def a_rows(q):
        return pl.ds(pl.multiple_of(q * ra, ra), ra)

    def level_rows(q):
        total = jnp.zeros((ra, 128), F32)
        for k in range(nk):
            rows = pl.ds(pl.multiple_of(k * nj + q * ra, ra), ra)
            total = total + proj[rows, :] * t32[k:k + 1, :]
        return total

    def a1(k):
        return remote(glf.at[ppeer(k)], r1.at[sp], a1_s.at[k], a1_r.at[sp], p_id(k))

    def a1_in(k):
        return remote(glf.at[ppeer(k)], r1.at[ppeer(k)], a1_s.at[k], a1_r.at[ppeer(k)], p_id(k))

    for k in range(1, NS):
        glf[ppeer(k)] = level_rows(ppeer(k))
        a1(k).start()
    r1[sp] = level_rows(sp)

    for k in range(nk):
        g1[pl.ds(k, 1), :] = jnp.sum(proj[pl.ds(k * nj, nj), :] * l32, axis=0, keepdims=True)
    g1[pl.ds(nk, 8), :] = sq[:, :128] + sq[:, 128:]

    def b1(k):
        return remote(g1, q1.at[a], b1_s.at[k], b1_r.at[a], a_id(k))

    def b1_in(k):
        return remote(g1, q1.at[apeer(k)], b1_s.at[k], b1_r.at[apeer(k)], a_id(k))

    for k in range(1, NA):
        b1(k).start()
    q1[a] = g1[...]

    for s in (6, 7):
        relay(s).wait_recv()
    zs[0] = part[1, 0] + rbuf[0] + rbuf[1]
    rs_x0.start()

    rs_x(1).wait_recv()
    for s in (2, 3):
        zs[s] = part[0, s] + xbuf[s]
        short(s).start()
    rs_x1.wait_recv()
    zs[1] = part[0, 1] + xbuf[1]
    for h in range(2):
        half(h).start()

    for k in range(1, NS):
        a1_in(k).wait_recv()
    total = r1[0]
    for q in range(1, NS):
        total = total + r1[q]
    m2[...] = total

    def a2(s):
        return remote(m2, r2.at[t], a2_s.at[s], a2_r.at[t], {"tm": zpeer(s)})

    def a2_in(s):
        return remote(m2, r2.at[zpeer(s)], a2_s.at[s], a2_r.at[zpeer(s)], {"tm": zpeer(s)})

    for s in range(1, NT):
        a2(s).start()
    r2[t] = m2[...]

    for k in range(1, NA):
        b1_in(k).wait_recv()
    total = q1[0]
    for q in range(1, NA):
        total = total + q1[q]
    g2[...] = total

    def b2(k):
        return remote(g2, q2.at[xc], b2_s.at[k], b2_r.at[xc], x_id(k))

    def b2_in(k):
        return remote(g2, q2.at[xpeer(k)], b2_s.at[k], b2_r.at[xpeer(k)], x_id(k))

    for k in range(1, NX * NV):
        b2(k).start()
    q2[xc] = g2[...]

    rs_x(2).wait_recv()
    for s in (4, 5):
        h = s - 4
        short(s - 2).wait_recv()
        half(h).wait_recv()
        zs[s] = part[0, s] + xbuf[s] + tbuf[h]
        rows = pl.ds(64 * h, 64)
        zs[s, rows] += hbuf[h]
        last(s).start()

    for h in range(2):
        ag_half(h).wait_send()
        near(6 + h).wait_send()
        relay(6 + h).wait_send()
    for p in range(NT // 2):
        for h in range(2):
            ag_x(p, h).wait_send()
    for s in range(2, NT):
        ag_z(s).wait_send()
    for k in range(1, NA):
        b1(k).wait_send()
    for k in range(1, NS):
        a1(k).wait_send()
    rs_x1.wait_send()
    for p in (1, 2):
        rs_x(p).wait_send()

    for k in range(1, NX * NV):
        b2_in(k).wait_recv()
    total = q2[0]
    for q in range(1, NX * NV):
        total = total + q2[q]
    gt_ref[...] = total[0:nk, :] * scales[2]
    m3[...] = total[nk:nk + 8, :]

    def b3(s):
        return remote(m3, r3.at[t], b3_s.at[s], b3_r.at[t], {"tm": zpeer(s)})

    def b3_in(s):
        return remote(m3, r3.at[zpeer(s)], b3_s.at[s], b3_r.at[zpeer(s)], {"tm": zpeer(s)})

    for s in range(1, NT):
        b3(s).start()
    r3[t] = m3[...]

    for s in range(1, NT):
        a2_in(s).wait_recv()
    total = r2[0]
    for q in range(1, NT):
        total = total + r2[q]
    glo[a_rows(sp), :] = total * scales[1]

    def a3(k):
        return remote(glo.at[a_rows(sp)], glo.at[a_rows(sp)], a3_s.at[k], a3_r.at[sp], p_id(k))

    def a3_in(k):
        rows = a_rows(ppeer(k))
        return remote(glo.at[rows], glo.at[rows], a3_s.at[k], a3_r.at[ppeer(k)], p_id(k))

    for k in range(1, NS):
        a3(k).start()

    rs_x0.wait_recv()
    total = part[0, 0] + xbuf[0]
    for s in (6, 7, 4, 5):
        remote(zs.at[s], zbuf.at[s], rz_s.at[s], rz_r.at[s], partner).wait_recv()
        total = total + zbuf[s]
    gs_ref[...] = total.T * scales[0]

    for s in range(1, NT):
        b3_in(s).wait_recv()
    total = r3[0]
    for q in range(1, NT):
        total = total + r3[q]
    loss_ref[0, 0] = jnp.sum(total) * scales[3]
    for k in range(1, NX * NV):
        b2(k).wait_send()
    for s in range(1, NT):
        a2(s).wait_send()
    rs_x0.wait_send()
    for h in range(2):
        half(h).wait_send()
        short(2 + h).wait_send()
    for h in range(2):
        last(4 + h).wait_send()
    for s in range(1, NT):
        b3(s).wait_send()
    for k in range(1, NS):
        a3_in(k).wait_recv()
    gl_ref[...] = glo[...]

    for k in range(1, NS):
        a3(k).wait_send()


def on_device(field, factor_space, factor_level, factor_time):
    nk, nj, ni = field.shape
    own = factor_space.shape[0]
    kj = nk * nj
    count_i, count_j, count_k = own * NS * NV * NT, nj * NV, nk * NT
    scales = (
        1.0 / (count_j * count_k) ** 0.5,
        1.0 / (count_i * count_k) ** 0.5,
        1.0 / (count_i * count_j) ** 0.5,
        0.5 / (count_i * count_j * count_k),
    )
    dma = pltpu.SemaphoreType.DMA
    vmem = pl.BlockSpec(memory_space=pltpu.VMEM)
    inputs = [pltpu.with_memory_space_constraint(x, pltpu.HBM)
              for x in (field, factor_space, factor_level, factor_time)]
    gs, gl, gt, loss = pl.pallas_call(
        functools.partial(kernel, scales),
        out_shape=(
            jax.ShapeDtypeStruct((own, 128), F32),
            jax.ShapeDtypeStruct((nj, 128), F32),
            jax.ShapeDtypeStruct((nk, 128), F32),
            jax.ShapeDtypeStruct((1, 1), F32),
        ),
        in_specs=[pl.BlockSpec(memory_space=pltpu.HBM)] * 4,
        out_specs=(vmem, vmem, vmem, pl.BlockSpec(memory_space=pltpu.SMEM)),
        scratch_shapes=[
            pltpu.VMEM((own, 128), BF16),
            pltpu.VMEM((nj, 128), BF16),
            pltpu.VMEM((nk, 128), BF16),
            pltpu.VMEM((NT, nk, nj, 256), BF16),
            pltpu.VMEM((NV, NT // 2, 256, 128), BF16),
            pltpu.VMEM((kj, 128), BF16),
            pltpu.VMEM((128, kj), BF16),
            pltpu.VMEM((kj, 256), BF16),
            pltpu.VMEM((kj, 128), F32),
            pltpu.VMEM((8, 256), F32),
            pltpu.VMEM((NV, NT, 128, 128), F32),
            pltpu.VMEM((NT, 128, 128), F32),
            pltpu.VMEM((NT, 128, 128), F32),
            pltpu.VMEM((NT, 128, 128), F32),
            pltpu.VMEM((2, 128, 128), F32),
            pltpu.VMEM((2, 128, 128), F32),
            pltpu.VMEM((2, 64, 128), F32),
            pltpu.VMEM((NS, nj // NS, 128), F32),
            pltpu.VMEM((NS, nj // NS, 128), F32),
            pltpu.VMEM((nk + 8, 128), F32),
            pltpu.VMEM((NA, nk + 8, 128), F32),
            pltpu.VMEM((nj // NS, 128), F32),
            pltpu.VMEM((NT, nj // NS, 128), F32),
            pltpu.VMEM((nk + 8, 128), F32),
            pltpu.VMEM((NX * NV, nk + 8, 128), F32),
            pltpu.VMEM((8, 128), F32),
            pltpu.VMEM((NT, 8, 128), F32),
            pltpu.VMEM((nj, 128), F32),
            dma((3,)), dma((NT, 2)), dma((2,)), dma((2,)),
            dma((NT,)), dma((NT,)), dma((NT // 2, 2)), dma((NT // 2, 2)),
            dma((NT // 2,)), dma((NT // 2,)), dma((NT,)), dma((NT,)),
            dma((2,)), dma((2,)), dma((2,)), dma((2,)),
            dma((NS,)), dma((NS,)), dma((NA,)), dma((NA,)),
            dma((NT,)), dma((NT,)), dma((NX * NV,)), dma((NX * NV,)),
            dma((NS,)), dma((NS,)), dma((NT,)), dma((NT,)),
        ],
        compiler_params=pltpu.CompilerParams(collective_id=0, has_side_effects=True,
                                             vmem_limit_bytes=40 * 2**20),
    )(*inputs)
    return gs, gl, gt, loss.reshape(())


def solution(mesh):
    placed = (
        P("tm", "var", "space"),
        P(("space", "var", "tm"), None),
        P("var", None),
        P("tm", None),
    )
    return jax.shard_map(
        on_device,
        mesh=mesh,
        in_specs=placed,
        out_specs=(P(("space", "var", "tm"), None), P("var", None), P("tm", None), P()),
        check_vma=False,
    )
```

```python
import functools

import jax
import jax.numpy as jnp
from jax import lax
from jax.experimental import pallas as pl
from jax.experimental.pallas import tpu as pltpu
from jax.sharding import PartitionSpec as P

MESH = pl.DeviceIdType.MESH
BF16, F32 = jnp.bfloat16, jnp.float32
NS, NV, NT = 16, 2, 8
NA, NX = 8, 2
CHUNK = 512


def offset_of(s):
    if isinstance(s, int):
        return (0, 4, 3, 5, 2, 6, 1, 7)[s]
    mag = NT // 2 - s // 2
    signed = jnp.where(s % 2 == 0, mag, NT - mag)
    return jnp.where(s == 0, 0, jnp.where(s == 1, NT // 2, signed))


def mirror(s):
    return (0, 1, 3, 2, 5, 4, 7, 6)[s]


def kernel(scales, field, s_hbm, l_hbm, t_hbm, gs_ref, gl_ref, gt_ref, loss_ref,
           s_ref, l_ref, t_ref, fbuf, ag, khat, khat_t, mb, proj, sq, part, xbuf, zs, zbuf, rbuf, tbuf,
           glf, r1, g1, q1, m2, r2, g2, q2, m3, r3, glo,
           isem, fsem, agh_s, agh_r, agz_s, agz_r, agx_s, agx_r, rx_s, rx_r, rz_s, rz_r, rr_s, rr_r,
           a1_s, a1_r, b1_s, b1_r, a2_s, a2_r, b2_s, b2_r, a3_s, a3_r, b3_s, b3_r):
    sp, v, t = lax.axis_index("space"), lax.axis_index("var"), lax.axis_index("tm")
    xh, a = sp // NA, sp % NA
    xc = xh * NV + v
    partner = {"var": 1 - v}
    nk, nj = t_ref.shape[0], l_ref.shape[0]

    def zpeer(s):
        return lax.rem(t + offset_of(s), NT)

    def apeer(k):
        return lax.rem(a + k, NA)

    def a_id(k):
        return {"space": xh * NA + apeer(k)}

    def ppeer(k):
        return lax.rem(sp + k, NS)

    def p_id(k):
        return {"space": ppeer(k)}

    def xpeer(k):
        return lax.rem(xc + k, NX * NV)

    def x_id(k):
        return {"space": xpeer(k) // NV * NA + a, "var": xpeer(k) % NV}

    def remote(src, dst, send, recv, dev):
        return pltpu.make_async_remote_copy(src_ref=src, dst_ref=dst, send_sem=send, recv_sem=recv,
                                            device_id=dev, device_id_type=MESH)

    small = [pltpu.make_async_copy(x, y, isem.at[i])
             for i, (x, y) in enumerate(((l_hbm, l_ref), (t_hbm, t_ref), (s_hbm, s_ref)))]
    for copy in small:
        copy.start()

    barrier = pltpu.get_barrier_semaphore()
    for s in range(1, NT):
        pl.semaphore_signal(barrier, inc=1, device_id={"tm": zpeer(s)}, device_id_type=MESH)
    pl.semaphore_signal(barrier, inc=1, device_id=partner, device_id_type=MESH)
    pl.semaphore_signal(barrier, inc=1, device_id={"space": (1 - xh) * NA + a, "var": 1 - v}, device_id_type=MESH)
    for k in range(1, NS):
        pl.semaphore_signal(barrier, inc=1, device_id=p_id(k), device_id_type=MESH)

    def turn_of(i):
        if isinstance(i, int):
            return ((0, 2), (0, 1), (1, 2), (0, 3), (0, 0), (1, 1), (1, 3), (1, 0))[i]
        w = jnp.where((i == 2) | (i >= 5), 1, 0)
        p = jnp.where((i == 3) | (i == 6), 3, 0)
        p = jnp.where((i == 1) | (i == 5), 1, p)
        return w, jnp.where((i == 0) | (i == 2), 2, p)

    def field_copy(i, h):
        w, p = turn_of(i)
        own = v + w * (1 - 2 * v)
        owner = own * NT + lax.rem(t + offset_of(2 * p + h), NT)
        cols = pl.ds(pl.multiple_of(owner * 128, 128), 128)
        return pltpu.make_async_copy(field.at[:, :, cols], fbuf.at[i, :, :, pl.ds(h * 128, 128)], fsem.at[i, h])

    for i in range(NT):
        for h in range(2):
            field_copy(i, h).start()

    for copy in small:
        copy.wait()
    l32 = l_ref[...].astype(F32)
    t32 = t_ref[...].astype(F32)
    l32t, t32t = l32.T, t32.T
    for k in range(nk):
        khat[pl.ds(k * nj, nj), :] = (l32 * t32[k:k + 1, :]).astype(BF16)
        khat_t[:, pl.ds(k * nj, nj)] = (l32t * t32t[:, k:k + 1]).astype(BF16)
    ag[0, 0, pl.ds(0, 128), :] = s_ref[...]
    proj[...] = jnp.zeros_like(proj)
    sq[...] = jnp.zeros_like(sq)

    pl.semaphore_wait(barrier, NT - 1 + 2 + NS - 1)

    def slot(w, s):
        return ag.at[w, s // 2, pl.ds((s % 2) * 128, 128)]

    def ag_z(s):
        return remote(s_ref, slot(0, mirror(s)), agz_s.at[s], agz_r.at[mirror(s)], {"tm": zpeer(s)})

    def ag_z_in(s):
        return remote(s_ref, slot(0, s), agz_s.at[s], agz_r.at[s], {"tm": zpeer(s)})

    def ag_x(p, h):
        rows = pl.ds(h * 128, 128)
        return remote(ag.at[0, p, rows], ag.at[1, p, rows], agx_s.at[p, h], agx_r.at[p, h], partner)

    remote(s_ref, slot(1, 0), agx_s.at[0, 0], agx_r.at[0, 0], partner).start()
    for s in (4, 5, 2, 3, 6, 7):
        ag_z(s).start()

    def ag_half(h):
        return remote(ag.at[0, 2, pl.ds(128 * h + 64 * h, 64)], ag.at[0, 0, pl.ds(128 + 64 * h, 64)],
                      agh_s.at[h], agh_r.at[h], {"tm": lax.rem(t + (6, 2)[h], NT)})

    def pass_on(p, h):
        s = 2 * p + h
        rows = pl.ds(h * 128, 128)
        remote(s_ref, ag.at[0, p, rows], agz_s.at[s], agz_r.at[s], partner).wait_recv()
        ag_x(p, h).start()

    def rs_x(p):
        two = pl.ds(2 * p, 2)
        return remote(part.at[1, two], xbuf.at[two], rx_s.at[p], rx_r.at[p], partner)

    rs_x1 = remote(part.at[1, 1], xbuf.at[1], rx_s.at[0], rx_r.at[0], partner)
    rs_x0 = remote(zs.at[0], xbuf.at[0], rx_s.at[3], rx_r.at[3], partner)

    def z_to(k):
        return {"tm": lax.rem(t + k, NT)}

    def near(s):
        m = mirror(s)
        return remote(part.at[0, s], zbuf.at[m], rz_s.at[s], rz_r.at[m], z_to(offset_of(s)))

    def relay(s):
        return remote(part.at[1, s], rbuf.at[s - 6], rr_s.at[s - 6], rr_r.at[s - 6], z_to(offset_of(s)))

    def far():
        return remote(zs.at[1], zbuf.at[1], rz_s.at[1], rz_r.at[1], z_to(4))

    def short(s):
        return remote(zs.at[s], tbuf.at[s - 2], rz_s.at[s], rz_r.at[s], z_to((1, 7)[s - 2]))

    def last(s):
        m = mirror(s)
        return remote(zs.at[s], zbuf.at[m], rz_s.at[s], rz_r.at[m], z_to(offset_of(s)))

    def turn(i, carry):
        w, p = turn_of(i)

        @pl.when((i == 1) | (i == 3))
        def _():
            for h in range(2):
                pass_on(i, h)

        @pl.when(i == 4)
        def _():
            for h in range(2):
                ag_half(h).wait_recv()
            ag_x(0, 1).start()

        for h in range(2):
            field_copy(i, h).wait()

        @pl.when(w == 1)
        def _():
            for h in range(2):
                ag_x(p, h).wait_recv()

        sb = ag[w, p]
        per = CHUNK // nj
        acc = sq[...]
        for c in range(nk // per):
            rows = pl.ds(c * CHUNK, CHUNK)
            model = lax.dot_general(khat[rows, :], sb, (((1,), (1,)), ((), ())), preferred_element_type=F32)
            data = fbuf[i, pl.ds(c * per, per), :, :].reshape(CHUNK, 256).astype(F32)
            misfit = model - data
            acc = acc + jnp.sum((misfit * misfit).reshape(CHUNK // 8, 8, 256), axis=0)
            mb[rows, :] = misfit.astype(BF16)
        sq[...] = acc
        grad = jnp.dot(khat_t[...], mb[...], preferred_element_type=F32)
        part[w, 2 * p] = grad[:, :128]
        part[w, 2 * p + 1] = grad[:, 128:]

        @pl.when((i == 2) | (i == 5))
        def _():
            rs_x(p).start()

        @pl.when(i == 3)
        def _():
            for s in (6, 7):
                near(s).start()

        @pl.when(i == 6)
        def _():
            for s in (6, 7):
                relay(s).start()

        @pl.when(i == 7)
        def _():
            rs_x1.start()

        proj[...] += jnp.dot(mb[...], sb, preferred_element_type=F32)
        return carry

    for h in range(2):
        ag_z_in(4 + h).wait_recv()
        ag_half(h).start()
        ag_x(2, h).start()
    lax.fori_loop(0, NT, turn, 0)

    ra = nj // NT

    def a_rows(q):
        return pl.ds(pl.multiple_of(q * ra, ra), ra)

    def level_rows(q):
        total = jnp.zeros((ra, 128), F32)
        for k in range(nk):
            rows = pl.ds(pl.multiple_of(k * nj + q * ra, ra), ra)
            total = total + proj[rows, :] * t32[k:k + 1, :]
        return total

    def a1(k):
        return remote(glf.at[zpeer(k)], r1.at[t], a1_s.at[k], a1_r.at[t], {"tm": zpeer(k)})

    def a1_in(k):
        return remote(glf.at[zpeer(k)], r1.at[zpeer(k)], a1_s.at[k], a1_r.at[zpeer(k)], {"tm": zpeer(k)})

    for k in range(1, NT):
        glf[zpeer(k)] = level_rows(zpeer(k))
        a1(k).start()
    r1[t] = level_rows(t)

    for k in range(nk):
        g1[pl.ds(k, 1), :] = jnp.sum(proj[pl.ds(k * nj, nj), :] * l32, axis=0, keepdims=True)
    g1[pl.ds(nk, 8), :] = sq[:, :128] + sq[:, 128:]

    def b1(k):
        return remote(g1, q1.at[a], b1_s.at[k], b1_r.at[a], a_id(k))

    def b1_in(k):
        return remote(g1, q1.at[apeer(k)], b1_s.at[k], b1_r.at[apeer(k)], a_id(k))

    for k in range(1, NA):
        b1(k).start()
    q1[a] = g1[...]

    for s in (6, 7):
        relay(s).wait_recv()
    zs[0] = part[1, 0] + rbuf[0] + rbuf[1]
    rs_x0.start()

    rs_x(1).wait_recv()
    for s in (2, 3):
        zs[s] = part[0, s] + xbuf[s]
        short(s).start()
    rs_x1.wait_recv()
    zs[1] = part[0, 1] + xbuf[1]
    far().start()

    for k in range(1, NT):
        a1_in(k).wait_recv()
    total = r1[0]
    for q in range(1, NT):
        total = total + r1[q]
    m2[...] = total

    def a2(k):
        return remote(m2, r2.at[sp], a2_s.at[k], a2_r.at[sp], p_id(k))

    def a2_in(k):
        return remote(m2, r2.at[ppeer(k)], a2_s.at[k], a2_r.at[ppeer(k)], p_id(k))

    for k in range(1, NS):
        a2(k).start()
    r2[sp] = m2[...]

    for k in range(1, NA):
        b1_in(k).wait_recv()
    total = q1[0]
    for q in range(1, NA):
        total = total + q1[q]
    g2[...] = total

    def b2(k):
        return remote(g2, q2.at[xc], b2_s.at[k], b2_r.at[xc], x_id(k))

    def b2_in(k):
        return remote(g2, q2.at[xpeer(k)], b2_s.at[k], b2_r.at[xpeer(k)], x_id(k))

    for k in range(1, NX * NV):
        b2(k).start()
    q2[xc] = g2[...]

    rs_x(2).wait_recv()
    for s in (4, 5):
        h = s - 4
        short(s - 2).wait_recv()
        zs[s] = part[0, s] + xbuf[s] + tbuf[h]
        last(s).start()

    for h in range(2):
        ag_half(h).wait_send()
        near(6 + h).wait_send()
        relay(6 + h).wait_send()
    for p in range(NT // 2):
        for h in range(2):
            ag_x(p, h).wait_send()
    for s in range(2, NT):
        ag_z(s).wait_send()
    for k in range(1, NA):
        b1(k).wait_send()
    for k in range(1, NT):
        a1(k).wait_send()
    rs_x1.wait_send()
    for p in (1, 2):
        rs_x(p).wait_send()

    for k in range(1, NX * NV):
        b2_in(k).wait_recv()
    total = q2[0]
    for q in range(1, NX * NV):
        total = total + q2[q]
    gt_ref[...] = total[0:nk, :] * scales[2]
    m3[...] = total[nk:nk + 8, :]

    def b3(s):
        return remote(m3, r3.at[t], b3_s.at[s], b3_r.at[t], {"tm": zpeer(s)})

    def b3_in(s):
        return remote(m3, r3.at[zpeer(s)], b3_s.at[s], b3_r.at[zpeer(s)], {"tm": zpeer(s)})

    for s in range(1, NT):
        b3(s).start()
    r3[t] = m3[...]

    for k in range(1, NS):
        a2_in(k).wait_recv()
    total = r2[0]
    for q in range(1, NS):
        total = total + r2[q]
    glo[a_rows(t), :] = total * scales[1]

    def a3(k):
        return remote(glo.at[a_rows(t)], glo.at[a_rows(t)], a3_s.at[k], a3_r.at[t], {"tm": zpeer(k)})

    def a3_in(k):
        rows = a_rows(zpeer(k))
        return remote(glo.at[rows], glo.at[rows], a3_s.at[k], a3_r.at[zpeer(k)], {"tm": zpeer(k)})

    for k in range(1, NT):
        a3(k).start()

    rs_x0.wait_recv()
    total = part[0, 0] + xbuf[0]
    for s in (6, 7, 4, 5, 1):
        remote(zs.at[s], zbuf.at[s], rz_s.at[s], rz_r.at[s], partner).wait_recv()
        total = total + zbuf[s]
    gs_ref[...] = total.T * scales[0]

    for s in range(1, NT):
        b3_in(s).wait_recv()
    total = r3[0]
    for q in range(1, NT):
        total = total + r3[q]
    loss_ref[0, 0] = jnp.sum(total) * scales[3]
    for k in range(1, NX * NV):
        b2(k).wait_send()
    for k in range(1, NS):
        a2(k).wait_send()
    rs_x0.wait_send()
    far().wait_send()
    for h in range(2):
        short(2 + h).wait_send()
    for h in range(2):
        last(4 + h).wait_send()
    for s in range(1, NT):
        b3(s).wait_send()
    for k in range(1, NT):
        a3_in(k).wait_recv()
    gl_ref[...] = glo[...]

    for k in range(1, NT):
        a3(k).wait_send()


def on_device(field, factor_space, factor_level, factor_time):
    nk, nj, ni = field.shape
    own = factor_space.shape[0]
    kj = nk * nj
    count_i, count_j, count_k = own * NS * NV * NT, nj * NV, nk * NT
    scales = (
        1.0 / (count_j * count_k) ** 0.5,
        1.0 / (count_i * count_k) ** 0.5,
        1.0 / (count_i * count_j) ** 0.5,
        0.5 / (count_i * count_j * count_k),
    )
    dma = pltpu.SemaphoreType.DMA
    vmem = pl.BlockSpec(memory_space=pltpu.VMEM)
    inputs = [pltpu.with_memory_space_constraint(x, pltpu.HBM)
              for x in (field, factor_space, factor_level, factor_time)]
    gs, gl, gt, loss = pl.pallas_call(
        functools.partial(kernel, scales),
        out_shape=(
            jax.ShapeDtypeStruct((own, 128), F32),
            jax.ShapeDtypeStruct((nj, 128), F32),
            jax.ShapeDtypeStruct((nk, 128), F32),
            jax.ShapeDtypeStruct((1, 1), F32),
        ),
        in_specs=[pl.BlockSpec(memory_space=pltpu.HBM)] * 4,
        out_specs=(vmem, vmem, vmem, pl.BlockSpec(memory_space=pltpu.SMEM)),
        scratch_shapes=[
            pltpu.VMEM((own, 128), BF16),
            pltpu.VMEM((nj, 128), BF16),
            pltpu.VMEM((nk, 128), BF16),
            pltpu.VMEM((NT, nk, nj, 256), BF16),
            pltpu.VMEM((NV, NT // 2, 256, 128), BF16),
            pltpu.VMEM((kj, 128), BF16),
            pltpu.VMEM((128, kj), BF16),
            pltpu.VMEM((kj, 256), BF16),
            pltpu.VMEM((kj, 128), F32),
            pltpu.VMEM((8, 256), F32),
            pltpu.VMEM((NV, NT, 128, 128), F32),
            pltpu.VMEM((NT, 128, 128), F32),
            pltpu.VMEM((NT, 128, 128), F32),
            pltpu.VMEM((NT, 128, 128), F32),
            pltpu.VMEM((2, 128, 128), F32),
            pltpu.VMEM((2, 128, 128), F32),
            pltpu.VMEM((NT, nj // NT, 128), F32),
            pltpu.VMEM((NT, nj // NT, 128), F32),
            pltpu.VMEM((nk + 8, 128), F32),
            pltpu.VMEM((NA, nk + 8, 128), F32),
            pltpu.VMEM((nj // NT, 128), F32),
            pltpu.VMEM((NS, nj // NT, 128), F32),
            pltpu.VMEM((nk + 8, 128), F32),
            pltpu.VMEM((NX * NV, nk + 8, 128), F32),
            pltpu.VMEM((8, 128), F32),
            pltpu.VMEM((NT, 8, 128), F32),
            pltpu.VMEM((nj, 128), F32),
            dma((3,)), dma((NT, 2)), dma((2,)), dma((2,)),
            dma((NT,)), dma((NT,)), dma((NT // 2, 2)), dma((NT // 2, 2)),
            dma((NT // 2,)), dma((NT // 2,)), dma((NT,)), dma((NT,)),
            dma((2,)), dma((2,)),
            dma((NT,)), dma((NT,)), dma((NA,)), dma((NA,)),
            dma((NS,)), dma((NS,)), dma((NX * NV,)), dma((NX * NV,)),
            dma((NT,)), dma((NT,)), dma((NT,)), dma((NT,)),
        ],
        compiler_params=pltpu.CompilerParams(collective_id=0, has_side_effects=True,
                                             vmem_limit_bytes=40 * 2**20),
    )(*inputs)
    return gs, gl, gt, loss.reshape(())


def solution(mesh):
    placed = (
        P("tm", "var", "space"),
        P(("space", "var", "tm"), None),
        P("var", None),
        P("tm", None),
    )
    return jax.shard_map(
        on_device,
        mesh=mesh,
        in_specs=placed,
        out_specs=(P(("space", "var", "tm"), None), P("var", None), P("tm", None), P()),
        check_vma=False,
    )
```

```python
import functools

import jax
import jax.numpy as jnp
from jax import lax
from jax.experimental import pallas as pl
from jax.experimental.pallas import tpu as pltpu
from jax.sharding import PartitionSpec as P

MESH = pl.DeviceIdType.MESH
BF16, F32 = jnp.bfloat16, jnp.float32
NS, NV, NT = 16, 2, 8
NA, NX = 8, 2
CHUNK = 512


def offset_of(s):
    if isinstance(s, int):
        return (0, 4, 3, 5, 2, 6, 1, 7)[s]
    mag = NT // 2 - s // 2
    signed = jnp.where(s % 2 == 0, mag, NT - mag)
    return jnp.where(s == 0, 0, jnp.where(s == 1, NT // 2, signed))


def mirror(s):
    return (0, 1, 3, 2, 5, 4, 7, 6)[s]


def kernel(scales, field, s_hbm, l_hbm, t_hbm, gs_ref, gl_ref, gt_ref, loss_ref,
           s_ref, l_ref, t_ref, fbuf, ag, khat, khat_t, mb, proj, sq, part, xbuf, zs, zbuf, rbuf, tbuf,
           glf, r1, g1, q1, m2, r2, g2, q2, m3, r3, glo,
           isem, fsem, agh_s, agh_r, agz_s, agz_r, agx_s, agx_r, rx_s, rx_r, rz_s, rz_r, rr_s, rr_r,
           a1_s, a1_r, b1_s, b1_r, a2_s, a2_r, b2_s, b2_r, a3_s, a3_r, b3_s, b3_r):
    sp, v, t = lax.axis_index("space"), lax.axis_index("var"), lax.axis_index("tm")
    xh, a = sp // NA, sp % NA
    xc = xh * NV + v
    partner = {"var": 1 - v}
    nk, nj = t_ref.shape[0], l_ref.shape[0]

    def zpeer(s):
        return lax.rem(t + offset_of(s), NT)

    def apeer(k):
        return lax.rem(a + k, NA)

    def a_id(k):
        return {"space": xh * NA + apeer(k)}

    def ppeer(k):
        return lax.rem(sp + k, NS)

    def p_id(k):
        return {"space": ppeer(k)}

    def xpeer(k):
        return lax.rem(xc + k, NX * NV)

    def x_id(k):
        return {"space": xpeer(k) // NV * NA + a, "var": xpeer(k) % NV}

    def remote(src, dst, send, recv, dev):
        return pltpu.make_async_remote_copy(src_ref=src, dst_ref=dst, send_sem=send, recv_sem=recv,
                                            device_id=dev, device_id_type=MESH)

    small = [pltpu.make_async_copy(x, y, isem.at[i])
             for i, (x, y) in enumerate(((l_hbm, l_ref), (t_hbm, t_ref), (s_hbm, s_ref)))]
    for copy in small:
        copy.start()

    barrier = pltpu.get_barrier_semaphore()
    for s in range(1, NT):
        pl.semaphore_signal(barrier, inc=1, device_id={"tm": zpeer(s)}, device_id_type=MESH)
    pl.semaphore_signal(barrier, inc=1, device_id=partner, device_id_type=MESH)
    pl.semaphore_signal(barrier, inc=1, device_id={"space": (1 - xh) * NA + a, "var": 1 - v}, device_id_type=MESH)
    for k in range(1, NS):
        pl.semaphore_signal(barrier, inc=1, device_id=p_id(k), device_id_type=MESH)

    def turn_of(i):
        if isinstance(i, int):
            return ((0, 2), (0, 3), (1, 2), (0, 1), (0, 0), (1, 3), (1, 1), (1, 0))[i]
        w = jnp.where((i == 2) | (i >= 5), 1, 0)
        p = jnp.where((i == 1) | (i == 5), 3, 0)
        p = jnp.where((i == 3) | (i == 6), 1, p)
        return w, jnp.where((i == 0) | (i == 2), 2, p)

    def field_copy(i, h):
        w, p = turn_of(i)
        own = v + w * (1 - 2 * v)
        owner = own * NT + lax.rem(t + offset_of(2 * p + h), NT)
        cols = pl.ds(pl.multiple_of(owner * 128, 128), 128)
        return pltpu.make_async_copy(field.at[:, :, cols], fbuf.at[i, :, :, pl.ds(h * 128, 128)], fsem.at[i, h])

    for i in range(NT):
        for h in range(2):
            field_copy(i, h).start()

    for copy in small:
        copy.wait()
    l32 = l_ref[...].astype(F32)
    t32 = t_ref[...].astype(F32)
    l32t, t32t = l32.T, t32.T
    for k in range(nk):
        khat[pl.ds(k * nj, nj), :] = (l32 * t32[k:k + 1, :]).astype(BF16)
        khat_t[:, pl.ds(k * nj, nj)] = (l32t * t32t[:, k:k + 1]).astype(BF16)
    ag[0, 0, pl.ds(0, 128), :] = s_ref[...]
    proj[...] = jnp.zeros_like(proj)
    sq[...] = jnp.zeros_like(sq)

    pl.semaphore_wait(barrier, NT - 1 + 2 + NS - 1)

    def slot(w, s):
        return ag.at[w, s // 2, pl.ds((s % 2) * 128, 128)]

    def ag_z(s):
        return remote(s_ref, slot(0, mirror(s)), agz_s.at[s], agz_r.at[mirror(s)], {"tm": zpeer(s)})

    def ag_z_in(s):
        return remote(s_ref, slot(0, s), agz_s.at[s], agz_r.at[s], {"tm": zpeer(s)})

    def ag_x(p, h):
        rows = pl.ds(h * 128, 128)
        return remote(ag.at[0, p, rows], ag.at[1, p, rows], agx_s.at[p, h], agx_r.at[p, h], partner)

    remote(s_ref, slot(1, 0), agx_s.at[0, 0], agx_r.at[0, 0], partner).start()
    for s in (4, 5, 6, 7, 2, 3):
        ag_z(s).start()

    def ag_half(h):
        return remote(ag.at[0, 2, pl.ds(128 * h + 64 * h, 64)], ag.at[0, 0, pl.ds(128 + 64 * h, 64)],
                      agh_s.at[h], agh_r.at[h], {"tm": lax.rem(t + (6, 2)[h], NT)})

    def pass_on(p, h):
        s = 2 * p + h
        rows = pl.ds(h * 128, 128)
        remote(s_ref, ag.at[0, p, rows], agz_s.at[s], agz_r.at[s], partner).wait_recv()
        ag_x(p, h).start()

    def rs_x(p):
        two = pl.ds(2 * p, 2)
        return remote(part.at[1, two], xbuf.at[two], rx_s.at[p], rx_r.at[p], partner)

    rs_x1 = remote(part.at[1, 1], xbuf.at[1], rx_s.at[0], rx_r.at[0], partner)
    rs_x0 = remote(zs.at[0], xbuf.at[0], rx_s.at[3], rx_r.at[3], partner)

    def z_to(k):
        return {"tm": lax.rem(t + k, NT)}

    def near(s):
        m = mirror(s)
        return remote(part.at[0, s], zbuf.at[m], rz_s.at[s], rz_r.at[m], z_to(offset_of(s)))

    def relay(s):
        return remote(part.at[1, s], rbuf.at[s - 6], rr_s.at[s - 6], rr_r.at[s - 6], z_to(offset_of(s)))

    def far():
        return remote(zs.at[1], zbuf.at[1], rz_s.at[1], rz_r.at[1], z_to(4))

    def short(s):
        return remote(zs.at[s], tbuf.at[s - 2], rz_s.at[s], rz_r.at[s], z_to((1, 7)[s - 2]))

    def last(s):
        m = mirror(s)
        return remote(zs.at[s], zbuf.at[m], rz_s.at[s], rz_r.at[m], z_to(offset_of(s)))

    def turn(i, carry):
        w, p = turn_of(i)

        @pl.when((i == 1) | (i == 3))
        def _():
            for h in range(2):
                pass_on(4 - i, h)

        @pl.when(i == 4)
        def _():
            for h in range(2):
                ag_half(h).wait_recv()
            ag_x(0, 1).start()

        for h in range(2):
            field_copy(i, h).wait()

        @pl.when(w == 1)
        def _():
            for h in range(2):
                ag_x(p, h).wait_recv()

        sb = ag[w, p]
        per = CHUNK // nj
        acc = sq[...]
        for c in range(nk // per):
            rows = pl.ds(c * CHUNK, CHUNK)
            model = lax.dot_general(khat[rows, :], sb, (((1,), (1,)), ((), ())), preferred_element_type=F32)
            data = fbuf[i, pl.ds(c * per, per), :, :].reshape(CHUNK, 256).astype(F32)
            misfit = model - data
            acc = acc + jnp.sum((misfit * misfit).reshape(CHUNK // 8, 8, 256), axis=0)
            mb[rows, :] = misfit.astype(BF16)
        sq[...] = acc
        grad = jnp.dot(khat_t[...], mb[...], preferred_element_type=F32)
        part[w, 2 * p] = grad[:, :128]
        part[w, 2 * p + 1] = grad[:, 128:]

        @pl.when((i == 2) | (i == 6))
        def _():
            rs_x(p).start()

        @pl.when(i == 1)
        def _():
            for s in (6, 7):
                near(s).start()

        @pl.when(i == 5)
        def _():
            for s in (6, 7):
                relay(s).start()

        @pl.when(i == 7)
        def _():
            rs_x1.start()

        proj[...] += jnp.dot(mb[...], sb, preferred_element_type=F32)
        return carry

    for h in range(2):
        ag_z_in(4 + h).wait_recv()
        ag_half(h).start()
        ag_x(2, h).start()
    lax.fori_loop(0, NT, turn, 0)

    ra = nj // NT

    def a_rows(q):
        return pl.ds(pl.multiple_of(q * ra, ra), ra)

    def level_rows(q):
        total = jnp.zeros((ra, 128), F32)
        for k in range(nk):
            rows = pl.ds(pl.multiple_of(k * nj + q * ra, ra), ra)
            total = total + proj[rows, :] * t32[k:k + 1, :]
        return total

    def a1(k):
        return remote(glf.at[zpeer(k)], r1.at[t], a1_s.at[k], a1_r.at[t], {"tm": zpeer(k)})

    def a1_in(k):
        return remote(glf.at[zpeer(k)], r1.at[zpeer(k)], a1_s.at[k], a1_r.at[zpeer(k)], {"tm": zpeer(k)})

    for k in range(1, NT):
        glf[zpeer(k)] = level_rows(zpeer(k))
        a1(k).start()
    r1[t] = level_rows(t)

    for k in range(nk):
        g1[pl.ds(k, 1), :] = jnp.sum(proj[pl.ds(k * nj, nj), :] * l32, axis=0, keepdims=True)
    g1[pl.ds(nk, 8), :] = sq[:, :128] + sq[:, 128:]

    def b1(k):
        return remote(g1, q1.at[a], b1_s.at[k], b1_r.at[a], a_id(k))

    def b1_in(k):
        return remote(g1, q1.at[apeer(k)], b1_s.at[k], b1_r.at[apeer(k)], a_id(k))

    for k in range(1, NA):
        b1(k).start()
    q1[a] = g1[...]

    for s in (6, 7):
        relay(s).wait_recv()
    zs[0] = part[1, 0] + rbuf[0] + rbuf[1]
    rs_x0.start()

    rs_x(1).wait_recv()
    for s in (2, 3):
        zs[s] = part[0, s] + xbuf[s]
        short(s).start()
    rs_x1.wait_recv()
    zs[1] = part[0, 1] + xbuf[1]
    far().start()

    for k in range(1, NT):
        a1_in(k).wait_recv()
    total = r1[0]
    for q in range(1, NT):
        total = total + r1[q]
    m2[...] = total

    def a2(k):
        return remote(m2, r2.at[sp], a2_s.at[k], a2_r.at[sp], p_id(k))

    def a2_in(k):
        return remote(m2, r2.at[ppeer(k)], a2_s.at[k], a2_r.at[ppeer(k)], p_id(k))

    for k in range(1, NS):
        a2(k).start()
    r2[sp] = m2[...]

    for k in range(1, NA):
        b1_in(k).wait_recv()
    total = q1[0]
    for q in range(1, NA):
        total = total + q1[q]
    g2[...] = total

    def b2(k):
        return remote(g2, q2.at[xc], b2_s.at[k], b2_r.at[xc], x_id(k))

    def b2_in(k):
        return remote(g2, q2.at[xpeer(k)], b2_s.at[k], b2_r.at[xpeer(k)], x_id(k))

    for k in range(1, NX * NV):
        b2(k).start()
    q2[xc] = g2[...]

    rs_x(2).wait_recv()
    for s in (4, 5):
        h = s - 4
        short(s - 2).wait_recv()
        zs[s] = part[0, s] + xbuf[s] + tbuf[h]
        last(s).start()

    for h in range(2):
        ag_half(h).wait_send()
        near(6 + h).wait_send()
        relay(6 + h).wait_send()
    for p in range(NT // 2):
        for h in range(2):
            ag_x(p, h).wait_send()
    for s in range(2, NT):
        ag_z(s).wait_send()
    for k in range(1, NA):
        b1(k).wait_send()
    for k in range(1, NT):
        a1(k).wait_send()
    rs_x1.wait_send()
    for p in (1, 2):
        rs_x(p).wait_send()

    for k in range(1, NX * NV):
        b2_in(k).wait_recv()
    total = q2[0]
    for q in range(1, NX * NV):
        total = total + q2[q]
    gt_ref[...] = total[0:nk, :] * scales[2]
    m3[...] = total[nk:nk + 8, :]

    def b3(s):
        return remote(m3, r3.at[t], b3_s.at[s], b3_r.at[t], {"tm": zpeer(s)})

    def b3_in(s):
        return remote(m3, r3.at[zpeer(s)], b3_s.at[s], b3_r.at[zpeer(s)], {"tm": zpeer(s)})

    for s in range(1, NT):
        b3(s).start()
    r3[t] = m3[...]

    for k in range(1, NS):
        a2_in(k).wait_recv()
    total = r2[0]
    for q in range(1, NS):
        total = total + r2[q]
    glo[a_rows(t), :] = total * scales[1]

    def a3(k):
        return remote(glo.at[a_rows(t)], glo.at[a_rows(t)], a3_s.at[k], a3_r.at[t], {"tm": zpeer(k)})

    def a3_in(k):
        rows = a_rows(zpeer(k))
        return remote(glo.at[rows], glo.at[rows], a3_s.at[k], a3_r.at[zpeer(k)], {"tm": zpeer(k)})

    for k in range(1, NT):
        a3(k).start()

    rs_x0.wait_recv()
    total = part[0, 0] + xbuf[0]
    for s in (6, 7, 4, 5, 1):
        remote(zs.at[s], zbuf.at[s], rz_s.at[s], rz_r.at[s], partner).wait_recv()
        total = total + zbuf[s]
    gs_ref[...] = total.T * scales[0]

    for s in range(1, NT):
        b3_in(s).wait_recv()
    total = r3[0]
    for q in range(1, NT):
        total = total + r3[q]
    loss_ref[0, 0] = jnp.sum(total) * scales[3]
    for k in range(1, NX * NV):
        b2(k).wait_send()
    for k in range(1, NS):
        a2(k).wait_send()
    rs_x0.wait_send()
    far().wait_send()
    for h in range(2):
        short(2 + h).wait_send()
    for h in range(2):
        last(4 + h).wait_send()
    for s in range(1, NT):
        b3(s).wait_send()
    for k in range(1, NT):
        a3_in(k).wait_recv()
    gl_ref[...] = glo[...]

    for k in range(1, NT):
        a3(k).wait_send()


def on_device(field, factor_space, factor_level, factor_time):
    nk, nj, ni = field.shape
    own = factor_space.shape[0]
    kj = nk * nj
    count_i, count_j, count_k = own * NS * NV * NT, nj * NV, nk * NT
    scales = (
        1.0 / (count_j * count_k) ** 0.5,
        1.0 / (count_i * count_k) ** 0.5,
        1.0 / (count_i * count_j) ** 0.5,
        0.5 / (count_i * count_j * count_k),
    )
    dma = pltpu.SemaphoreType.DMA
    vmem = pl.BlockSpec(memory_space=pltpu.VMEM)
    inputs = [pltpu.with_memory_space_constraint(x, pltpu.HBM)
              for x in (field, factor_space, factor_level, factor_time)]
    gs, gl, gt, loss = pl.pallas_call(
        functools.partial(kernel, scales),
        out_shape=(
            jax.ShapeDtypeStruct((own, 128), F32),
            jax.ShapeDtypeStruct((nj, 128), F32),
            jax.ShapeDtypeStruct((nk, 128), F32),
            jax.ShapeDtypeStruct((1, 1), F32),
        ),
        in_specs=[pl.BlockSpec(memory_space=pltpu.HBM)] * 4,
        out_specs=(vmem, vmem, vmem, pl.BlockSpec(memory_space=pltpu.SMEM)),
        scratch_shapes=[
            pltpu.VMEM((own, 128), BF16),
            pltpu.VMEM((nj, 128), BF16),
            pltpu.VMEM((nk, 128), BF16),
            pltpu.VMEM((NT, nk, nj, 256), BF16),
            pltpu.VMEM((NV, NT // 2, 256, 128), BF16),
            pltpu.VMEM((kj, 128), BF16),
            pltpu.VMEM((128, kj), BF16),
            pltpu.VMEM((kj, 256), BF16),
            pltpu.VMEM((kj, 128), F32),
            pltpu.VMEM((8, 256), F32),
            pltpu.VMEM((NV, NT, 128, 128), F32),
            pltpu.VMEM((NT, 128, 128), F32),
            pltpu.VMEM((NT, 128, 128), F32),
            pltpu.VMEM((NT, 128, 128), F32),
            pltpu.VMEM((2, 128, 128), F32),
            pltpu.VMEM((2, 128, 128), F32),
            pltpu.VMEM((NT, nj // NT, 128), F32),
            pltpu.VMEM((NT, nj // NT, 128), F32),
            pltpu.VMEM((nk + 8, 128), F32),
            pltpu.VMEM((NA, nk + 8, 128), F32),
            pltpu.VMEM((nj // NT, 128), F32),
            pltpu.VMEM((NS, nj // NT, 128), F32),
            pltpu.VMEM((nk + 8, 128), F32),
            pltpu.VMEM((NX * NV, nk + 8, 128), F32),
            pltpu.VMEM((8, 128), F32),
            pltpu.VMEM((NT, 8, 128), F32),
            pltpu.VMEM((nj, 128), F32),
            dma((3,)), dma((NT, 2)), dma((2,)), dma((2,)),
            dma((NT,)), dma((NT,)), dma((NT // 2, 2)), dma((NT // 2, 2)),
            dma((NT // 2,)), dma((NT // 2,)), dma((NT,)), dma((NT,)),
            dma((2,)), dma((2,)),
            dma((NT,)), dma((NT,)), dma((NA,)), dma((NA,)),
            dma((NS,)), dma((NS,)), dma((NX * NV,)), dma((NX * NV,)),
            dma((NT,)), dma((NT,)), dma((NT,)), dma((NT,)),
        ],
        compiler_params=pltpu.CompilerParams(collective_id=0, has_side_effects=True,
                                             vmem_limit_bytes=40 * 2**20),
    )(*inputs)
    return gs, gl, gt, loss.reshape(())


def solution(mesh):
    placed = (
        P("tm", "var", "space"),
        P(("space", "var", "tm"), None),
        P("var", None),
        P("tm", None),
    )
    return jax.shard_map(
        on_device,
        mesh=mesh,
        in_specs=placed,
        out_specs=(P(("space", "var", "tm"), None), P("var", None), P("tm", None), P()),
        check_vma=False,
    )
```

```python
import functools

import jax
import jax.numpy as jnp
from jax import lax
from jax.experimental import pallas as pl
from jax.experimental.pallas import tpu as pltpu
from jax.sharding import PartitionSpec as P

MESH = pl.DeviceIdType.MESH
BF16, F32 = jnp.bfloat16, jnp.float32
NS, NV, NT = 16, 2, 8
NA, NX = 8, 2
CHUNK = 512


def offset_of(s):
    if isinstance(s, int):
        return (0, 4, 3, 5, 2, 6, 1, 7)[s]
    mag = NT // 2 - s // 2
    signed = jnp.where(s % 2 == 0, mag, NT - mag)
    return jnp.where(s == 0, 0, jnp.where(s == 1, NT // 2, signed))


def mirror(s):
    return (0, 1, 3, 2, 5, 4, 7, 6)[s]


def kernel(scales, field, s_hbm, l_hbm, t_hbm, gs_ref, gl_ref, gt_ref, loss_ref,
           s_ref, l_ref, t_ref, fbuf, ag, khat, khat_t, mb, proj, sq, part, xbuf, zs, zbuf, rbuf, tbuf,
           glf, r1, g1, q1, m2, r2, g2, q2, m3, r3, glo,
           isem, fsem, agh_s, agh_r, agz_s, agz_r, agx_s, agx_r, rx_s, rx_r, rz_s, rz_r, rr_s, rr_r,
           a1_s, a1_r, b1_s, b1_r, a2_s, a2_r, b2_s, b2_r, a3_s, a3_r, b3_s, b3_r):
    sp, v, t = lax.axis_index("space"), lax.axis_index("var"), lax.axis_index("tm")
    xh, a = sp // NA, sp % NA
    xc = xh * NV + v
    partner = {"var": 1 - v}
    nk, nj = t_ref.shape[0], l_ref.shape[0]

    def zpeer(s):
        return lax.rem(t + offset_of(s), NT)

    def apeer(k):
        return lax.rem(a + k, NA)

    def a_id(k):
        return {"space": xh * NA + apeer(k)}

    def ppeer(k):
        return lax.rem(sp + k, NS)

    def p_id(k):
        return {"space": ppeer(k)}

    def xpeer(k):
        return lax.rem(xc + k, NX * NV)

    def x_id(k):
        return {"space": xpeer(k) // NV * NA + a, "var": xpeer(k) % NV}

    def remote(src, dst, send, recv, dev):
        return pltpu.make_async_remote_copy(src_ref=src, dst_ref=dst, send_sem=send, recv_sem=recv,
                                            device_id=dev, device_id_type=MESH)

    small = [pltpu.make_async_copy(x, y, isem.at[i])
             for i, (x, y) in enumerate(((l_hbm, l_ref), (t_hbm, t_ref), (s_hbm, s_ref)))]
    for copy in small:
        copy.start()

    barrier = pltpu.get_barrier_semaphore()
    for s in range(1, NT):
        pl.semaphore_signal(barrier, inc=1, device_id={"tm": zpeer(s)}, device_id_type=MESH)
    pl.semaphore_signal(barrier, inc=1, device_id=partner, device_id_type=MESH)
    pl.semaphore_signal(barrier, inc=1, device_id={"space": (1 - xh) * NA + a, "var": 1 - v}, device_id_type=MESH)
    for k in range(1, NS):
        pl.semaphore_signal(barrier, inc=1, device_id=p_id(k), device_id_type=MESH)

    def turn_of(i):
        if isinstance(i, int):
            return ((0, 2), (0, 3), (1, 2), (0, 1), (0, 0), (1, 3), (1, 1), (1, 0))[i]
        w = jnp.where((i == 2) | (i >= 5), 1, 0)
        p = jnp.where((i == 1) | (i == 5), 3, 0)
        p = jnp.where((i == 3) | (i == 6), 1, p)
        return w, jnp.where((i == 0) | (i == 2), 2, p)

    def field_copy(i, h):
        w, p = turn_of(i)
        own = v + w * (1 - 2 * v)
        owner = own * NT + lax.rem(t + offset_of(2 * p + h), NT)
        cols = pl.ds(pl.multiple_of(owner * 128, 128), 128)
        return pltpu.make_async_copy(field.at[:, :, cols], fbuf.at[i, :, :, pl.ds(h * 128, 128)], fsem.at[i, h])

    for i in range(NT):
        for h in range(2):
            field_copy(i, h).start()

    for copy in small:
        copy.wait()
    l32 = l_ref[...].astype(F32)
    t32 = t_ref[...].astype(F32)
    l32t, t32t = l32.T, t32.T
    for k in range(nk):
        khat[pl.ds(k * nj, nj), :] = (l32 * t32[k:k + 1, :]).astype(BF16)
        khat_t[:, pl.ds(k * nj, nj)] = (l32t * t32t[:, k:k + 1]).astype(BF16)
    ag[0, 0, pl.ds(0, 128), :] = s_ref[...]
    proj[...] = jnp.zeros_like(proj)
    sq[...] = jnp.zeros_like(sq)

    pl.semaphore_wait(barrier, NT - 1 + 2 + NS - 1)

    def slot(w, s):
        return ag.at[w, s // 2, pl.ds((s % 2) * 128, 128)]

    def ag_z(s):
        return remote(s_ref, slot(0, mirror(s)), agz_s.at[s], agz_r.at[mirror(s)], {"tm": zpeer(s)})

    def ag_z_in(s):
        return remote(s_ref, slot(0, s), agz_s.at[s], agz_r.at[s], {"tm": zpeer(s)})

    def ag_x(p, h):
        rows = pl.ds(h * 128, 128)
        return remote(ag.at[0, p, rows], ag.at[1, p, rows], agx_s.at[p, h], agx_r.at[p, h], partner)

    remote(s_ref, slot(1, 0), agx_s.at[0, 0], agx_r.at[0, 0], partner).start()
    for s in (4, 5, 6, 7, 2, 3):
        ag_z(s).start()

    def ag_half(h):
        return remote(ag.at[0, 2, pl.ds(128 * h + 64 * h, 64)], ag.at[0, 0, pl.ds(128 + 64 * h, 64)],
                      agh_s.at[h], agh_r.at[h], {"tm": lax.rem(t + (6, 2)[h], NT)})

    def pass_on(p, h):
        s = 2 * p + h
        rows = pl.ds(h * 128, 128)
        remote(s_ref, ag.at[0, p, rows], agz_s.at[s], agz_r.at[s], partner).wait_recv()
        ag_x(p, h).start()

    def rs_x(p):
        two = pl.ds(2 * p, 2)
        return remote(part.at[1, two], xbuf.at[two], rx_s.at[p], rx_r.at[p], partner)

    rs_x1 = remote(part.at[1, 1], xbuf.at[1], rx_s.at[0], rx_r.at[0], partner)
    rs_x0 = remote(zs.at[0], xbuf.at[0], rx_s.at[3], rx_r.at[3], partner)

    def z_to(k):
        return {"tm": lax.rem(t + k, NT)}

    def near(s):
        m = mirror(s)
        return remote(part.at[0, s], zbuf.at[m], rz_s.at[s], rz_r.at[m], z_to(offset_of(s)))

    def relay(s):
        return remote(part.at[1, s], rbuf.at[s - 6], rr_s.at[s - 6], rr_r.at[s - 6], z_to(offset_of(s)))

    def far():
        return remote(zs.at[1], zbuf.at[1], rz_s.at[1], rz_r.at[1], z_to(4))

    def short(s):
        return remote(zs.at[s], tbuf.at[s - 2], rz_s.at[s], rz_r.at[s], z_to((1, 7)[s - 2]))

    def last(s):
        m = mirror(s)
        return remote(zs.at[s], zbuf.at[m], rz_s.at[s], rz_r.at[m], z_to(offset_of(s)))

    def turn(i, carry):
        w, p = turn_of(i)

        @pl.when((i == 1) | (i == 3))
        def _():
            for h in range(2):
                pass_on(4 - i, h)

        @pl.when(i == 4)
        def _():
            for h in range(2):
                ag_half(h).wait_recv()
            ag_x(0, 1).start()

        for h in range(2):
            field_copy(i, h).wait()

        @pl.when(w == 1)
        def _():
            for h in range(2):
                ag_x(p, h).wait_recv()

        sb = ag[w, p]
        per = CHUNK // nj
        acc = sq[...]
        for c in range(nk // per):
            rows = pl.ds(c * CHUNK, CHUNK)
            model = lax.dot_general(khat[rows, :], sb, (((1,), (1,)), ((), ())), preferred_element_type=F32)
            data = fbuf[i, pl.ds(c * per, per), :, :].reshape(CHUNK, 256).astype(F32)
            misfit = model - data
            acc = acc + jnp.sum((misfit * misfit).reshape(CHUNK // 8, 8, 256), axis=0)
            mb[rows, :] = misfit.astype(BF16)
        sq[...] = acc
        grad = jnp.dot(khat_t[...], mb[...], preferred_element_type=F32)
        part[w, 2 * p] = grad[:, :128]
        part[w, 2 * p + 1] = grad[:, 128:]

        @pl.when((i == 2) | (i == 6))
        def _():
            rs_x(p).start()

        @pl.when(i == 1)
        def _():
            for s in (6, 7):
                near(s).start()

        @pl.when(i == 5)
        def _():
            for s in (6, 7):
                relay(s).start()

        @pl.when(i == 7)
        def _():
            rs_x1.start()

        proj[...] += jnp.dot(mb[...], sb, preferred_element_type=F32)
        return carry

    for h in range(2):
        ag_z_in(4 + h).wait_recv()
        ag_half(h).start()
        ag_x(2, h).start()
    lax.fori_loop(0, NT, turn, 0)

    ra = nj // NT

    def a_rows(q):
        return pl.ds(pl.multiple_of(q * ra, ra), ra)

    def level_rows(q):
        total = jnp.zeros((ra, 128), F32)
        for k in range(nk):
            rows = pl.ds(pl.multiple_of(k * nj + q * ra, ra), ra)
            total = total + proj[rows, :] * t32[k:k + 1, :]
        return total

    def a1(k):
        return remote(glf.at[zpeer(k)], r1.at[t], a1_s.at[k], a1_r.at[t], {"tm": zpeer(k)})

    def a1_in(k):
        return remote(glf.at[zpeer(k)], r1.at[zpeer(k)], a1_s.at[k], a1_r.at[zpeer(k)], {"tm": zpeer(k)})

    for k in range(1, NT):
        glf[zpeer(k)] = level_rows(zpeer(k))
        a1(k).start()
    r1[t] = level_rows(t)

    for k in range(nk):
        g1[pl.ds(k, 1), :] = jnp.sum(proj[pl.ds(k * nj, nj), :] * l32, axis=0, keepdims=True)
    g1[pl.ds(nk, 8), :] = sq[:, :128] + sq[:, 128:]

    def b1(k):
        return remote(g1, q1.at[a], b1_s.at[k], b1_r.at[a], a_id(k))

    def b1_in(k):
        return remote(g1, q1.at[apeer(k)], b1_s.at[k], b1_r.at[apeer(k)], a_id(k))

    for k in range(1, NA):
        b1(k).start()
    q1[a] = g1[...]

    for s in (6, 7):
        relay(s).wait_recv()
    zs[0] = part[1, 0] + rbuf[0] + rbuf[1]
    rs_x0.start()

    rs_x(1).wait_recv()
    for s in (2, 3):
        zs[s] = part[0, s] + xbuf[s]
        short(s).start()

    for k in range(1, NT):
        a1_in(k).wait_recv()
    total = r1[0]
    for q in range(1, NT):
        total = total + r1[q]
    m2[...] = total

    def a2(k):
        return remote(m2, r2.at[sp], a2_s.at[k], a2_r.at[sp], p_id(k))

    def a2_in(k):
        return remote(m2, r2.at[ppeer(k)], a2_s.at[k], a2_r.at[ppeer(k)], p_id(k))

    for k in range(1, NS):
        a2(k).start()
    r2[sp] = m2[...]
    rs_x1.wait_recv()
    zs[1] = part[0, 1] + xbuf[1]
    far().start()

    for k in range(1, NA):
        b1_in(k).wait_recv()
    total = q1[0]
    for q in range(1, NA):
        total = total + q1[q]
    g2[...] = total

    def b2(k):
        return remote(g2, q2.at[xc], b2_s.at[k], b2_r.at[xc], x_id(k))

    def b2_in(k):
        return remote(g2, q2.at[xpeer(k)], b2_s.at[k], b2_r.at[xpeer(k)], x_id(k))

    for k in range(1, NX * NV):
        b2(k).start()
    q2[xc] = g2[...]

    rs_x(2).wait_recv()
    for s in (4, 5):
        h = s - 4
        short(s - 2).wait_recv()
        zs[s] = part[0, s] + xbuf[s] + tbuf[h]
        last(s).start()

    for h in range(2):
        ag_half(h).wait_send()
        near(6 + h).wait_send()
        relay(6 + h).wait_send()
    for p in range(NT // 2):
        for h in range(2):
            ag_x(p, h).wait_send()
    for s in range(2, NT):
        ag_z(s).wait_send()
    for k in range(1, NA):
        b1(k).wait_send()
    for k in range(1, NT):
        a1(k).wait_send()
    rs_x1.wait_send()
    for p in (1, 2):
        rs_x(p).wait_send()

    for k in range(1, NX * NV):
        b2_in(k).wait_recv()
    total = q2[0]
    for q in range(1, NX * NV):
        total = total + q2[q]
    gt_ref[...] = total[0:nk, :] * scales[2]
    m3[...] = total[nk:nk + 8, :]

    def b3(s):
        return remote(m3, r3.at[t], b3_s.at[s], b3_r.at[t], {"tm": zpeer(s)})

    def b3_in(s):
        return remote(m3, r3.at[zpeer(s)], b3_s.at[s], b3_r.at[zpeer(s)], {"tm": zpeer(s)})

    for s in range(1, NT):
        b3(s).start()
    r3[t] = m3[...]

    for k in range(1, NS):
        a2_in(k).wait_recv()
    total = r2[0]
    for q in range(1, NS):
        total = total + r2[q]
    glo[a_rows(t), :] = total * scales[1]

    def a3(k):
        return remote(glo.at[a_rows(t)], glo.at[a_rows(t)], a3_s.at[k], a3_r.at[t], {"tm": zpeer(k)})

    def a3_in(k):
        rows = a_rows(zpeer(k))
        return remote(glo.at[rows], glo.at[rows], a3_s.at[k], a3_r.at[zpeer(k)], {"tm": zpeer(k)})

    for k in range(1, NT):
        a3(k).start()

    rs_x0.wait_recv()
    total = part[0, 0] + xbuf[0]
    for s in (6, 7, 4, 5, 1):
        remote(zs.at[s], zbuf.at[s], rz_s.at[s], rz_r.at[s], partner).wait_recv()
        total = total + zbuf[s]
    gs_ref[...] = total.T * scales[0]

    for s in range(1, NT):
        b3_in(s).wait_recv()
    total = r3[0]
    for q in range(1, NT):
        total = total + r3[q]
    loss_ref[0, 0] = jnp.sum(total) * scales[3]
    for k in range(1, NX * NV):
        b2(k).wait_send()
    for k in range(1, NS):
        a2(k).wait_send()
    rs_x0.wait_send()
    far().wait_send()
    for h in range(2):
        short(2 + h).wait_send()
    for h in range(2):
        last(4 + h).wait_send()
    for s in range(1, NT):
        b3(s).wait_send()
    for k in range(1, NT):
        a3_in(k).wait_recv()
    gl_ref[...] = glo[...]

    for k in range(1, NT):
        a3(k).wait_send()


def on_device(field, factor_space, factor_level, factor_time):
    nk, nj, ni = field.shape
    own = factor_space.shape[0]
    kj = nk * nj
    count_i, count_j, count_k = own * NS * NV * NT, nj * NV, nk * NT
    scales = (
        1.0 / (count_j * count_k) ** 0.5,
        1.0 / (count_i * count_k) ** 0.5,
        1.0 / (count_i * count_j) ** 0.5,
        0.5 / (count_i * count_j * count_k),
    )
    dma = pltpu.SemaphoreType.DMA
    vmem = pl.BlockSpec(memory_space=pltpu.VMEM)
    inputs = [pltpu.with_memory_space_constraint(x, pltpu.HBM)
              for x in (field, factor_space, factor_level, factor_time)]
    gs, gl, gt, loss = pl.pallas_call(
        functools.partial(kernel, scales),
        out_shape=(
            jax.ShapeDtypeStruct((own, 128), F32),
            jax.ShapeDtypeStruct((nj, 128), F32),
            jax.ShapeDtypeStruct((nk, 128), F32),
            jax.ShapeDtypeStruct((1, 1), F32),
        ),
        in_specs=[pl.BlockSpec(memory_space=pltpu.HBM)] * 4,
        out_specs=(vmem, vmem, vmem, pl.BlockSpec(memory_space=pltpu.SMEM)),
        scratch_shapes=[
            pltpu.VMEM((own, 128), BF16),
            pltpu.VMEM((nj, 128), BF16),
            pltpu.VMEM((nk, 128), BF16),
            pltpu.VMEM((NT, nk, nj, 256), BF16),
            pltpu.VMEM((NV, NT // 2, 256, 128), BF16),
            pltpu.VMEM((kj, 128), BF16),
            pltpu.VMEM((128, kj), BF16),
            pltpu.VMEM((kj, 256), BF16),
            pltpu.VMEM((kj, 128), F32),
            pltpu.VMEM((8, 256), F32),
            pltpu.VMEM((NV, NT, 128, 128), F32),
            pltpu.VMEM((NT, 128, 128), F32),
            pltpu.VMEM((NT, 128, 128), F32),
            pltpu.VMEM((NT, 128, 128), F32),
            pltpu.VMEM((2, 128, 128), F32),
            pltpu.VMEM((2, 128, 128), F32),
            pltpu.VMEM((NT, nj // NT, 128), F32),
            pltpu.VMEM((NT, nj // NT, 128), F32),
            pltpu.VMEM((nk + 8, 128), F32),
            pltpu.VMEM((NA, nk + 8, 128), F32),
            pltpu.VMEM((nj // NT, 128), F32),
            pltpu.VMEM((NS, nj // NT, 128), F32),
            pltpu.VMEM((nk + 8, 128), F32),
            pltpu.VMEM((NX * NV, nk + 8, 128), F32),
            pltpu.VMEM((8, 128), F32),
            pltpu.VMEM((NT, 8, 128), F32),
            pltpu.VMEM((nj, 128), F32),
            dma((3,)), dma((NT, 2)), dma((2,)), dma((2,)),
            dma((NT,)), dma((NT,)), dma((NT // 2, 2)), dma((NT // 2, 2)),
            dma((NT // 2,)), dma((NT // 2,)), dma((NT,)), dma((NT,)),
            dma((2,)), dma((2,)),
            dma((NT,)), dma((NT,)), dma((NA,)), dma((NA,)),
            dma((NS,)), dma((NS,)), dma((NX * NV,)), dma((NX * NV,)),
            dma((NT,)), dma((NT,)), dma((NT,)), dma((NT,)),
        ],
        compiler_params=pltpu.CompilerParams(collective_id=0, has_side_effects=True,
                                             vmem_limit_bytes=40 * 2**20),
    )(*inputs)
    return gs, gl, gt, loss.reshape(())


def solution(mesh):
    placed = (
        P("tm", "var", "space"),
        P(("space", "var", "tm"), None),
        P("var", None),
        P("tm", None),
    )
    return jax.shard_map(
        on_device,
        mesh=mesh,
        in_specs=placed,
        out_specs=(P(("space", "var", "tm"), None), P("var", None), P("tm", None), P()),
        check_vma=False,
    )
```
